256 devices in a mesh: pair: 32 (over y, z), virt: 8 (over x, core).
Axes of the slice: x: 4, y: 4, z: 8, core: 2. Of those that a mesh axis runs over, the one named last changes fastest.
Arguments:
- amplitudes: bfloat16 [16384, 16, 2048], P('pair', None, 'virt'), may hold values from -6 to 6
- integrals: bfloat16 [1024, 16, 2048], P(None, None, 'virt'), may hold values from -0.09375 to 0.09375
- mask: int32 [16384, 16, 16], P('pair', None, 'virt'), may hold values from 0 to 1
- slab: int32 [1], replicated, may hold values from 0 to 127
- owner: int32 [16384], replicated, may hold values from 0 to 16383, as said below
Outputs:
- symmetric: float32 [16384, 1024], P('pair', 'virt')
The draws below stay inside these ranges and needn't reach their ends.
Inputs may be any that keep to these rules, and one draw needn't show every extreme that they name: owner is a permutation; ids 2 q and 2 q + 1 are a pair ij and its mirror ji, never on the same index of pair; for any two indices of pair, at most 17 slots of one hold pairs whose mirror sits on the other, and this is reached.
All inputs are finite; a program needn't handle non-finite values.
Results may differ from the reference program's by a relative error of at most 0.0003.
Values sent between devices are 32-bit elements; how exact they have to be, the bound alone decides.
A program may use at most 64 MiB of HBM per device.

```python
import jax
import jax.numpy as jnp
from jax import lax

TILE = 128
NVIRT = 2048
CSLAB = 16
WA = 32
P_DEV = 512
NT = 16
NSLAB = 128
AB = 1024
PAIRS = 16384
N_PAIR = 32


def draw_mask(key, part):
    key = jax.random.fold_in(key, 5)
    key_one, key_two, key_three = jax.random.split(key, 3)
    device_level = jax.random.randint(key_one, (N_PAIR,), 1, 5)
    pair_level = jax.random.randint(key_two, (PAIRS,), 1, 5)
    density = jnp.repeat(device_level, P_DEV) * pair_level
    raw_draw = jax.random.randint(key_three, (PAIRS, NT, NT), 0, 40)
    return (raw_draw < density[:, None, None]).astype(jnp.int32)


def draw_owner(key, part):
    key = jax.random.fold_in(key, 9)
    key_one, key_two, key_three, key_four = jax.random.split(key, 4)
    slot_ids = jnp.arange(PAIRS, dtype=jnp.int32)
    device = slot_ids // P_DEV
    row_index = slot_ids % P_DEV
    offset = 1 + jax.random.permutation(key_one, P_DEV).astype(jnp.int32) % (N_PAIR - 1)
    partner = jnp.bitwise_xor(device, offset[row_index]) * P_DEV + row_index
    lower = slot_ids < partner
    shuffled = jax.random.permutation(key_two, PAIRS).astype(jnp.int32)
    scores = jnp.where(lower, shuffled, PAIRS + shuffled)
    ordering = jnp.argsort(scores).astype(jnp.int32)
    ranking = jnp.zeros((PAIRS,), jnp.int32).at[ordering].set(slot_ids)
    orbit_id = jnp.where(lower, ranking, ranking[partner])
    flip_bits = jax.random.randint(key_three, (PAIRS,), 0, 2)
    flip_bit = jnp.where(lower, flip_bits, flip_bits[partner])
    pair_id = 2 * orbit_id + jnp.where(lower, flip_bit, 1 - flip_bit)
    placing = jax.vmap(lambda sub_key: jax.random.permutation(sub_key, P_DEV))(jax.random.split(key_four, N_PAIR)).astype(jnp.int32)
    target = device * P_DEV + placing[device, row_index]
    return jnp.zeros((PAIRS,), jnp.int32).at[target].set(pair_id)


def block_levels(rng, extent, pieces, least, top_value):
    loudness, own = 1.0, jax.random.fold_in(rng, 6)
    for dim, parts in pieces:
        heights = jnp.exp(jax.random.uniform(jax.random.fold_in(own, dim), (parts,), jnp.float32, least / len(pieces), top_value / len(pieces)))
        loudness = loudness * jnp.repeat(heights, extent[dim] // parts).reshape([-1 if axis == dim else 1 for axis in range(len(extent))])
    return loudness


def scatter_about(stream_key, shape, spread, reach, cuts=(), kind=jnp.bfloat16):
    gain = block_levels(stream_key, shape, cuts, -0.22, 0.18) if cuts else 1.0
    array = jax.random.normal(stream_key, shape, jnp.float32) * spread * gain
    return jnp.minimum(jnp.maximum(array, -reach), reach).astype(kind)


def setup_inputs(seed: int = 0) -> dict:
    key_list = jax.random.split(jax.random.key(seed), 6)
    amplitudes = scatter_about(key_list[0], (PAIRS, CSLAB, NVIRT), 1.0, 6.0, ((0, 32), (2, 8)))
    integrals = scatter_about(key_list[1], (AB, CSLAB, NVIRT), (CSLAB * NVIRT // 7) ** -0.5, 0.09375, ((2, 8),))
    mask = draw_mask(jax.random.fold_in(key_list[5], 71), 0)
    slab = jax.random.randint(key_list[3], (1,), 0, NSLAB).astype(jnp.int32)
    owner = draw_owner(jax.random.fold_in(key_list[5], 71), 0)
    return {"amplitudes": amplitudes, "integrals": integrals, "mask": mask, "slab": slab, "owner": owner}


def reference(amplitudes, integrals, mask, slab, owner):
    slab_tile = ((slab[0] * CSLAB) // TILE).astype(jnp.int32)
    picked = lax.dynamic_index_in_dim(mask, slab_tile, axis=1, keepdims=False)
    select = jnp.repeat(picked, TILE, axis=1).astype(amplitudes.dtype)
    flat_ints = integrals.reshape(AB, CSLAB * NVIRT).T

    def one_block(inputs):
        block_amps, block_sel = inputs
        masked = block_amps * block_sel[:, None, :]
        return jnp.dot(masked.reshape(P_DEV, CSLAB * NVIRT), flat_ints, preferred_element_type=jnp.float32)

    ladder = lax.map(one_block, (amplitudes.reshape(N_PAIR, P_DEV, CSLAB, NVIRT), select.reshape(N_PAIR, P_DEV, NVIRT)))
    ladder = ladder.reshape(PAIRS, AB)
    slot_ids = jnp.arange(PAIRS, dtype=jnp.int32)
    inverse = jnp.zeros((PAIRS,), jnp.int32).at[owner].set(slot_ids)
    mirror = inverse[jnp.bitwise_xor(owner, 1)]
    turned = ladder.reshape(PAIRS, WA, WA).transpose(0, 2, 1).reshape(PAIRS, AB)
    return ladder + turned[mirror]
```

```python
import jax
import jax.numpy as jnp
from jax import lax
from jax.sharding import PartitionSpec as P

TILE = 128
CSLAB = 16
WA = 32
MOST = 17


def per_device(amplitudes, integrals, mask, slab, owner):
    rows_here = amplitudes.shape[0]
    local_tiles = mask.shape[2]
    slab_tile = slab[0] * CSLAB // TILE
    picked = lax.dynamic_index_in_dim(mask, slab_tile, axis=1, keepdims=False)
    picked_soft = picked.astype(amplitudes.dtype)
    width_here = amplitudes.shape[2]
    tiled = amplitudes.reshape(rows_here, CSLAB, local_tiles, width_here // local_tiles)
    masked = (tiled * picked_soft[:, None, :, None]).reshape(rows_here, CSLAB, width_here)
    partial_value = jnp.einsum("pcd,rcd->pr", masked, integrals, preferred_element_type=jnp.float32)
    count_virt = lax.axis_size("virt")
    count_pair = lax.axis_size("pair")
    share_size = WA // count_virt
    own_rows = lax.psum_scatter(partial_value, "virt", scatter_dimension=1, tiled=True)

    slot_ids = jnp.arange(owner.shape[0], dtype=jnp.int32)
    my_owner = lax.dynamic_slice_in_dim(owner, lax.axis_index("pair") * rows_here, rows_here)
    matches = owner[None, :] == jnp.bitwise_xor(my_owner, 1)[:, None]
    there = jnp.sum(jnp.where(matches, slot_ids[None, :] // rows_here, 0), axis=1)
    order = my_owner // 2
    before = (there[None, :] == there[:, None]) & (order[None, :] < order[:, None])
    place = there * MOST + jnp.sum(before.astype(jnp.int32), axis=1)
    places = jnp.arange(count_pair * MOST, dtype=jnp.int32)
    row_of = jnp.sum(jnp.where(place[:, None] == places[None, :], jnp.arange(rows_here, dtype=jnp.int32)[:, None], 0), axis=0)

    blocks = own_rows.reshape(rows_here, share_size, count_virt, share_size)
    turned = lax.all_to_all(blocks, "virt", split_axis=2, concat_axis=1, tiled=True)
    swapped = (
        turned.reshape(rows_here, WA, share_size)
        .transpose(0, 2, 1)
        .reshape(rows_here, share_size * WA)
    )
    sent = jnp.take(swapped, row_of, axis=0).reshape(count_pair, MOST, -1)
    came = lax.all_to_all(sent, "pair", split_axis=0, concat_axis=0, tiled=True)
    fetched = jnp.take(came.reshape(count_pair * MOST, -1), place, axis=0)
    return own_rows + fetched


def solution(mesh):
    return jax.shard_map(
        per_device,
        mesh=mesh,
        in_specs=(
            P("pair", None, "virt"),
            P(None, None, "virt"),
            P("pair", None, "virt"),
            P(),
            P(),
        ),
        out_specs=P("pair", "virt"),
        check_vma=False,
    )
```

```python
import functools

import jax
import jax.numpy as jnp
from jax import lax
from jax.experimental import pallas as pl
from jax.experimental.pallas import tpu as pltpu
from jax.sharding import PartitionSpec as P

MESH = pl.DeviceIdType.MESH
F32 = jnp.float32
BF16 = jnp.bfloat16
NX = 4
CORES = 2
VIRT = NX * CORES
BLOCK = 128
STEPS = (2, 1, 3, 0)
NT = (((1,), (1,)), ((), ()))
NN = (((1,), (0,)), ((), ()))


def split_two(value):
    high = value.astype(BF16)
    return high, (value - high.astype(F32)).astype(BF16)


def iota(shape, dim):
    return lax.broadcasted_iota(jnp.int32, shape, dim)


def flatten_into(dst, row, block, cs, width):
    flat = pltpu.einshape("pcd->p(cd)", block)
    for j in range(2):
        for c in range(cs):
            at = j * cs * 128 + c * 128
            dst[pl.ds(row, 16), at:at + 128] = flat[:, c * width + j * 128:c * width + (j + 1) * 128]


def kernel(
    n_pair, slots,
    amp, ints, mask_ref, slab_ref, owner_ref, out_ref,
    amp_raw, amp_flat, int_raw, int_flat, part, chip_in, acc, fwd, fin_left, fin_right,
    turned, sent, came, send_one, take_one,
    amp_sem, int_sem, chip_send, chip_recv, ring_send, ring_recv, turn_send, turn_recv, pair_send, pair_recv,
):
    rows, cs, width = amp_raw.shape
    tiles = rows // 128
    half_k = cs * 128
    half = BLOCK // 2
    me_p = lax.axis_index("pair")
    me_v = lax.axis_index("virt")
    x = me_v // CORES
    core = me_v % CORES
    other = me_v + 1 - 2 * core
    right = ((x + 1) % NX) * CORES + core
    left = ((x + NX - 1) % NX) * CORES + core

    def fetch_amp(q):
        at = pl.ds(q * 128, 128)
        return pltpu.make_async_copy(amp.at[at], amp_raw.at[at], amp_sem.at[q])

    def fetch_ints(k):
        to = (x + STEPS[k]) % NX
        at = pl.ds(pl.multiple_of(to * CORES * BLOCK, CORES * BLOCK), CORES * BLOCK)
        return pltpu.make_async_copy(ints.at[at], int_raw.at[k], int_sem.at[k])

    for q in range(tiles):
        fetch_amp(q).start()
    for k in range(NX):
        fetch_ints(k).start()

    barrier = pltpu.get_barrier_semaphore()

    @pl.loop(1, VIRT)
    def _(i):
        pl.semaphore_signal(barrier, inc=1, device_id=(me_p, (me_v + i) % VIRT), device_id_type=MESH)

    @pl.loop(1, n_pair)
    def _(i):
        pl.semaphore_signal(barrier, inc=1, device_id=((me_p + i) % n_pair, me_v), device_id_type=MESH)

    for q in range(tiles):
        fetch_amp(q).wait()

        @pl.loop(0, 8, unroll=4)
        def _(g):
            row = pl.multiple_of(q * 128 + g * 16, 16)
            flatten_into(amp_flat, row, amp_raw[pl.ds(row, 16)], cs, width)

    select = mask_ref[slab_ref[0] // 8].astype(F32)

    def multiply(k):
        fetch_ints(k).wait()
        flat = int_flat.at[k % 2]

        @pl.loop(0, CORES * VIRT, unroll=4)
        def _(g):
            base = (g // VIRT) * BLOCK + 4 * (g % VIRT)
            block = jnp.concatenate([int_raw[k, pl.ds(base + 32 * a, 4)] for a in range(4)], axis=0)
            flatten_into(flat, pl.multiple_of(g * 16, 16), block, cs, width)

        for nb in range(rows // 128 // 2 if rows > 128 else 1):
            ps = slice(nb * 256, nb * 256 + 256) if rows > 128 else slice(0, 128)
            one = lax.dot_general(flat[:, :half_k], amp_flat[ps, :half_k], NT, preferred_element_type=F32)
            two = lax.dot_general(flat[:, half_k:], amp_flat[ps, half_k:], NT, preferred_element_type=F32)
            value = one * select[0:1, ps] + two * select[1:2, ps]
            for c in range(CORES):
                part[k, c, :, ps] = value[c * BLOCK:(c + 1) * BLOCK]

    def chip_copy(k):
        return pltpu.make_async_remote_copy(
            src_ref=part.at[k, 1 - core], dst_ref=chip_in.at[k], send_sem=chip_send.at[k], recv_sem=chip_recv.at[k],
            device_id=(me_p, other), device_id_type=MESH)

    def ring_copy(i, src, dst, to):
        return pltpu.make_async_remote_copy(
            src_ref=src, dst_ref=dst, send_sem=ring_send.at[i], recv_sem=ring_recv.at[i],
            device_id=(me_p, to), device_id_type=MESH)

    low, high = pl.ds(0, half), pl.ds(half, half)
    ring = [
        ring_copy(0, acc.at[0, low], fwd.at[0], right),
        ring_copy(1, acc.at[0, high], fwd.at[1], left),
        ring_copy(2, acc.at[1, high], fin_left.at[high], right),
        ring_copy(3, acc.at[1, low], fin_left.at[low], right),
        ring_copy(4, acc.at[2, low], fin_right.at[low], left),
        ring_copy(5, acc.at[2, high], fin_right.at[high], left),
    ]

    def chip_sum(k):
        chip_copy(k).wait_recv()
        acc[k] = part[k, core] + chip_in[k]

    multiply(0)
    pl.semaphore_wait(barrier, VIRT - 1 + n_pair - 1)
    chip_copy(0).start()
    multiply(1)
    chip_copy(1).start()
    chip_sum(0)
    ring[0].start()
    ring[1].start()
    multiply(2)
    chip_copy(2).start()
    chip_sum(1)
    ring[2].start()
    ring[0].wait_recv()
    acc[1, low] += fwd[0]
    ring[3].start()
    multiply(3)
    chip_copy(3).start()
    chip_sum(2)
    ring[4].start()
    ring[1].wait_recv()
    acc[2, high] += fwd[1]
    ring[5].start()

    eye = iota((128, 128), 0) == iota((128, 128), 1)

    def as_column(row):
        return jnp.sum(jnp.where(eye, row, 0.0), axis=1, keepdims=True)

    def as_row(column):
        return jnp.sum(jnp.where(eye, column, 0.0), axis=0, keepdims=True)

    own_rows = [owner_ref[pl.ds(me_p * tiles + t, 1), :] for t in range(tiles)]
    wanted = [as_column((r ^ 1).astype(F32)).astype(jnp.int32) for r in own_rows]
    order_rows = [(r // 2).astype(F32) for r in own_rows]
    order_columns = [as_column(r) for r in order_rows]
    there_columns = []
    for t in range(tiles):
        want = jnp.broadcast_to(wanted[t], (128, 128))

        def look(g, found):
            return jnp.where(owner_ref[pl.ds(g, 1), :] == want, g // tiles, found)

        found = lax.fori_loop(0, n_pair * tiles, look, jnp.zeros((128, 128), jnp.int32), unroll=4)
        there_columns.append(jnp.max(found.astype(F32), axis=1, keepdims=True))
    there_rows = [as_row(c) for c in there_columns]
    places = []
    for t in range(tiles):
        before = jnp.zeros((128, 128), F32)
        for u in range(tiles):
            hit = (there_rows[u] == there_columns[t]) & (order_rows[u] < order_columns[t])
            before = before + jnp.where(hit, 1.0, 0.0)
        places.append(there_columns[t] * slots + jnp.sum(before, axis=1, keepdims=True))
    n_slots = n_pair * slots
    for t in range(tiles):
        at = slice(t * 128, (t + 1) * 128)
        column = places[t].astype(jnp.int32)
        take_one[at, :] = jnp.where(iota((128, n_slots), 1) == column, 1.0, 0.0).astype(BF16)
        row = as_row(places[t]).astype(jnp.int32)
        send_one[:, at] = jnp.where(iota((n_slots, 128), 0) == row, 1.0, 0.0).astype(BF16)

    chip_sum(3)
    for i in range(2, 6):
        ring[i].wait_recv()
    acc[3] = acc[3] + fin_left[...] + fin_right[...]

    def turn_copy(i):
        to = (me_v + i) % VIRT
        src = acc.at[3, pl.ds(pl.multiple_of(to * 16, 16), 16)]
        dst = turned.at[pl.ds(pl.multiple_of(me_v * 16, 16), 16)]
        return pltpu.make_async_remote_copy(
            src_ref=src, dst_ref=dst, send_sem=turn_send.at[i], recv_sem=turn_recv.at[i],
            device_id=(me_p, to), device_id_type=MESH)

    for i in range(1, VIRT):
        turn_copy(i).start()
    mine = pl.ds(pl.multiple_of(me_v * 16, 16), 16)
    turned[mine, :] = acc[3, mine, :]
    came[pl.ds(me_p, 1)] = jnp.zeros((1, slots, BLOCK), F32)

    own_high, own_low = split_two(acc[3])
    diagonal = jnp.where(iota((rows, rows), 0) == iota((rows, rows), 1), 1.0, 0.0).astype(BF16)
    own_pair = lax.dot_general(diagonal, jnp.concatenate([own_high, own_low], axis=0), NT, preferred_element_type=F32)
    source, target = iota((BLOCK, BLOCK), 0), iota((BLOCK, BLOCK), 1)
    group, first, second = source // 16, (source // 4) % 4, source % 4
    own_lanes = jnp.where(target == first * 32 + group * 4 + second, 1.0, 0.0).astype(BF16)
    mirror_lanes = jnp.where(target == second * 32 + group * 4 + first, 1.0, 0.0).astype(BF16)
    own_lanes = jnp.concatenate([own_lanes, own_lanes], axis=0)
    mirror_lanes = jnp.concatenate([mirror_lanes, mirror_lanes], axis=0)
    out_ref[...] = lax.dot_general(own_pair.astype(BF16), own_lanes, NN, preferred_element_type=F32)

    for i in range(1, VIRT):
        turn_copy(i).wait_recv()
    turned_high, turned_low = split_two(turned[...])
    both = lax.dot_general(
        send_one[...], jnp.concatenate([turned_high, turned_low], axis=0), NT, preferred_element_type=F32)
    sent[...] = (both[:, :BLOCK] + both[:, BLOCK:]).reshape(n_pair, slots, BLOCK)

    def pair_copy(i):
        to = (me_p + i) % n_pair
        return pltpu.make_async_remote_copy(
            src_ref=sent.at[to], dst_ref=came.at[me_p], send_sem=pair_send.at[i], recv_sem=pair_recv.at[i],
            device_id=(to, me_v), device_id_type=MESH)

    @pl.loop(1, n_pair)
    def _(i):
        pair_copy(i).start()

    @pl.loop(1, n_pair)
    def _(i):
        pair_copy(i).wait_recv()

    came_high, came_low = split_two(came[...].reshape(n_slots, BLOCK))
    fetched = lax.dot_general(
        take_one[...], jnp.concatenate([came_high, came_low], axis=1), NN, preferred_element_type=F32)
    out_ref[...] += lax.dot_general(fetched.astype(BF16), mirror_lanes, NN, preferred_element_type=F32)

    for k in range(NX):
        chip_copy(k).wait_send()
    for copy in ring:
        copy.wait_send()
    for i in range(1, VIRT):
        turn_copy(i).wait_send()

    @pl.loop(1, n_pair)
    def _(i):
        pair_copy(i).wait_send()


def per_device(n_pair, slots, amplitudes, integrals, mask, slab, owner):
    rows, cs, width = amplitudes.shape
    dma = pltpu.SemaphoreType.DMA
    n_slots = n_pair * slots
    half = BLOCK // 2
    return pl.pallas_call(
        functools.partial(kernel, n_pair, slots),
        out_shape=jax.ShapeDtypeStruct((rows, BLOCK), F32),
        in_specs=[
            pl.BlockSpec(memory_space=pl.ANY),
            pl.BlockSpec(memory_space=pl.ANY),
            pl.BlockSpec(memory_space=pltpu.VMEM),
            pl.BlockSpec(memory_space=pltpu.SMEM),
            pl.BlockSpec(memory_space=pltpu.VMEM),
        ],
        out_specs=pl.BlockSpec(memory_space=pltpu.VMEM),
        scratch_shapes=[
            pltpu.VMEM((rows, cs, width), BF16),
            pltpu.VMEM((rows, cs * width), BF16),
            pltpu.VMEM((NX, CORES * BLOCK, cs, width), BF16),
            pltpu.VMEM((2, CORES * BLOCK, cs * width), BF16),
            pltpu.VMEM((NX, CORES, BLOCK, rows), F32),
            pltpu.VMEM((NX, BLOCK, rows), F32),
            pltpu.VMEM((NX, BLOCK, rows), F32),
            pltpu.VMEM((2, half, rows), F32),
            pltpu.VMEM((BLOCK, rows), F32),
            pltpu.VMEM((BLOCK, rows), F32),
            pltpu.VMEM((BLOCK, rows), F32),
            pltpu.VMEM((n_pair, slots, BLOCK), F32),
            pltpu.VMEM((n_pair, slots, BLOCK), F32),
            pltpu.VMEM((n_slots, rows), BF16),
            pltpu.VMEM((rows, n_slots), BF16),
            dma((rows // 128,)),
            dma((NX,)),
            dma((NX,)),
            dma((NX,)),
            dma((6,)),
            dma((6,)),
            dma((VIRT,)),
            dma((VIRT,)),
            dma((n_pair,)),
            dma((n_pair,)),
        ],
        compiler_params=pltpu.CompilerParams(
            collective_id=0, has_side_effects=True, vmem_limit_bytes=56 * 2**20),
        cost_estimate=pl.CostEstimate(
            flops=2 * rows * cs * width * VIRT * BLOCK, bytes_accessed=13 * 2**20, transcendentals=0),
    )(amplitudes, integrals, jnp.transpose(mask, (1, 2, 0)), slab, owner.reshape(-1, 128))


def solution(mesh, slots=24):
    return jax.shard_map(
        functools.partial(per_device, mesh.shape["pair"], slots),
        mesh=mesh,
        in_specs=(
            P("pair", None, "virt"),
            P(None, None, "virt"),
            P("pair", None, "virt"),
            P(),
            P(),
        ),
        out_specs=P("pair", "virt"),
        check_vma=False,
    )
```

```python
import functools

import jax
import jax.numpy as jnp
from jax import lax
from jax.experimental import pallas as pl
from jax.experimental.pallas import tpu as pltpu
from jax.sharding import PartitionSpec as P

MESH = pl.DeviceIdType.MESH
F32 = jnp.float32
BF16 = jnp.bfloat16
NX = 4
CORES = 2
VIRT = NX * CORES
BLOCK = 128
PAD = 24
NT = (((1,), (1,)), ((), ()))
NN = (((1,), (0,)), ((), ()))


def split_two(value):
    high = value.astype(BF16)
    return high, (value - high.astype(F32)).astype(BF16)


def iota(shape, dim):
    return lax.broadcasted_iota(jnp.int32, shape, dim)


def flatten_into(dst, row, block, cs, width):
    flat = pltpu.einshape("pcd->p(cd)", block)
    for j in range(2):
        for c in range(cs):
            at = j * cs * 128 + c * 128
            dst[pl.ds(row, 16), at:at + 128] = flat[:, c * width + j * 128:c * width + (j + 1) * 128]


def kernel(
    n_pair, slots,
    amp, ints, mask_ref, slab_ref, owner_ref, own_ref, fetched_ref,
    amp_raw, amp_flat, int_raw, int_flat, part, chip_in, acc, fwd, fin_left, fin_right,
    turned, sent, came, send_one, take_one,
    amp_sem, int_sem, chip_send, chip_recv, ring_send, ring_recv, turn_send, turn_recv, pair_send, pair_recv,
):
    rows, cs, width = amp_raw.shape
    tiles = rows // 128
    half_k = cs * 128
    half = BLOCK // 2
    me_p = lax.axis_index("pair")
    me_v = lax.axis_index("virt")
    x = me_v // CORES
    core = me_v % CORES
    other = me_v + 1 - 2 * core
    right = ((x + 1) % NX) * CORES + core
    left = ((x + NX - 1) % NX) * CORES + core

    def fetch_amp(q):
        at = pl.ds(q * 128, 128)
        return pltpu.make_async_copy(amp.at[at], amp_raw.at[at], amp_sem.at[q])

    def fetch_ints(s):
        to = (x + (2, 1, 3, 0)[s]) % NX
        return pltpu.make_async_copy(ints.at[:, pl.ds(to * CORES * 4, CORES * 4)], int_raw.at[s], int_sem.at[s])

    for q in range(tiles):
        fetch_amp(q).start()
    fetch_ints(0).start()

    barrier = pltpu.get_barrier_semaphore()

    @pl.loop(1, VIRT)
    def _(i):
        pl.semaphore_signal(barrier, inc=1, device_id=(me_p, (me_v + i) % VIRT), device_id_type=MESH)

    @pl.loop(1, n_pair)
    def _(i):
        pl.semaphore_signal(barrier, inc=1, device_id=((me_p + i) % n_pair, me_v), device_id_type=MESH)

    for q in range(tiles):
        fetch_amp(q).wait()

        @pl.loop(0, 8, unroll=4)
        def _(g):
            row = pl.multiple_of(q * 128 + g * 16, 16)
            flatten_into(amp_flat, row, amp_raw[pl.ds(row, 16)], cs, width)

    for s in range(1, NX):
        fetch_ints(s).start()
    select = mask_ref[slab_ref[0] // 8].astype(F32)
    runs = (((0, 0), (0, 4)), ((1, 4), (2, 0)), ((1, 0), (2, 4)), ((3, 0), (3, 4)))

    def arrange(k):
        flat = int_flat.at[k % 2]
        for c in range(CORES):
            for r in range(2):
                s, first = runs[k][r]

                @pl.loop(0, 4, unroll=4)
                def _(g):
                    block = jnp.concatenate(
                        [int_raw[s, (first + g) * 4 + a, pl.ds(c * 4, 4)] for a in range(4)], axis=0)
                    row = pl.multiple_of((c * 8 + r * 4 + g) * 16, 16)
                    flatten_into(flat, row, block, cs, width)

    def multiply(k, nb):
        flat = int_flat.at[k % 2]
        span = min(256, rows)
        ps = slice(nb * span, (nb + 1) * span)
        one = lax.dot_general(flat[:, :half_k], amp_flat[ps, :half_k], NT, preferred_element_type=F32)
        two = lax.dot_general(flat[:, half_k:], amp_flat[ps, half_k:], NT, preferred_element_type=F32)
        value = one * select[0:1, ps] + two * select[1:2, ps]
        for c in range(CORES):
            part[k, c, :, ps] = value[c * BLOCK:(c + 1) * BLOCK]

    later = range(1, rows // min(256, rows))

    def chip_copy(k):
        return pltpu.make_async_remote_copy(
            src_ref=part.at[k, 1 - core], dst_ref=chip_in.at[k], send_sem=chip_send.at[k], recv_sem=chip_recv.at[k],
            device_id=(me_p, other), device_id_type=MESH)

    def ring_copy(i, src, dst, to):
        return pltpu.make_async_remote_copy(
            src_ref=src, dst_ref=dst, send_sem=ring_send.at[i], recv_sem=ring_recv.at[i],
            device_id=(me_p, to), device_id_type=MESH)

    low, high = pl.ds(0, half), pl.ds(half, half)
    ring = [
        ring_copy(0, acc.at[0, low], fwd.at[0], right),
        ring_copy(1, acc.at[0, high], fwd.at[1], left),
        ring_copy(2, acc.at[1, low], fin_left.at[high], right),
        ring_copy(3, acc.at[1, high], fin_right.at[low], left),
        ring_copy(4, acc.at[2, low], fin_left.at[low], right),
        ring_copy(5, acc.at[2, high], fin_right.at[high], left),
    ]

    def chip_sum(k):
        chip_copy(k).wait_recv()
        acc[k] = part[k, core] + chip_in[k]

    fetch_ints(0).wait()
    arrange(0)
    multiply(0, 0)
    for nb in later:
        multiply(0, nb)
    pl.semaphore_wait(barrier, VIRT - 1 + n_pair - 1)
    chip_copy(0).start()
    fetch_ints(1).wait()
    fetch_ints(2).wait()
    arrange(1)
    multiply(1, 0)
    chip_sum(0)
    ring[0].start()
    ring[1].start()
    for nb in later:
        multiply(1, nb)
    chip_copy(1).start()
    arrange(2)
    multiply(2, 0)
    chip_sum(1)
    ring[2].start()
    ring[3].start()
    for nb in later:
        multiply(2, nb)
    chip_copy(2).start()
    fetch_ints(3).wait()
    arrange(3)
    multiply(3, 0)
    chip_sum(2)
    for nb in later:
        multiply(3, nb)
    chip_copy(3).start()
    ring[0].wait_recv()
    acc[2, low] += fwd[0]
    ring[4].start()
    ring[1].wait_recv()
    acc[2, high] += fwd[1]
    ring[5].start()

    eye = iota((128, 128), 0) == iota((128, 128), 1)

    def as_column(row):
        return jnp.sum(jnp.where(eye, row, 0.0), axis=1, keepdims=True)

    def as_row(column):
        return jnp.sum(jnp.where(eye, column, 0.0), axis=0, keepdims=True)

    own_rows = [owner_ref[pl.ds(me_p * tiles + t, 1), :] for t in range(tiles)]
    wanted = [as_column((r ^ 1).astype(F32)).astype(jnp.int32) for r in own_rows]
    order_rows = [(r // 2).astype(F32) for r in own_rows]
    order_columns = [as_column(r) for r in order_rows]
    there_columns = []
    for t in range(tiles):
        want = jnp.broadcast_to(wanted[t], (128, 128))

        def look(g, found):
            return jnp.where(owner_ref[pl.ds(g, 1), :] == want, g // tiles, found)

        found = lax.fori_loop(0, n_pair * tiles, look, jnp.zeros((128, 128), jnp.int32), unroll=4)
        there_columns.append(jnp.max(found.astype(F32), axis=1, keepdims=True))
    there_rows = [as_row(c) for c in there_columns]
    places = []
    for t in range(tiles):
        before = jnp.zeros((128, 128), F32)
        for u in range(tiles):
            hit = (there_rows[u] == there_columns[t]) & (order_rows[u] < order_columns[t])
            before = before + jnp.where(hit, 1.0, 0.0)
        places.append(there_columns[t] * PAD + jnp.sum(before, axis=1, keepdims=True))
    n_slots = n_pair * PAD
    for t in range(tiles):
        at = slice(t * 128, (t + 1) * 128)
        column = places[t].astype(jnp.int32)
        take_one[at, :] = jnp.where(iota((128, n_slots), 1) == column, 1.0, 0.0).astype(BF16)
        row = as_row(places[t]).astype(jnp.int32)
        send_one[:, at] = jnp.where(iota((n_slots, 128), 0) == row, 1.0, 0.0).astype(BF16)

    came[pl.ds(me_p, 1)] = jnp.zeros((1, slots, BLOCK), F32)
    source, target = iota((BLOCK, BLOCK), 0), iota((BLOCK, BLOCK), 1)
    group, first, second = source // 16, (source // 4) % 4, source % 4
    own_lanes = jnp.where(target == first * 32 + group * 4 + second, 1.0, 0.0).astype(BF16)
    mirror_lanes = jnp.where(target == second * 32 + group * 4 + first, 1.0, 0.0).astype(BF16)
    own_lanes = jnp.concatenate([own_lanes, own_lanes], axis=0)
    mirror_lanes = jnp.concatenate([mirror_lanes, mirror_lanes], axis=0)
    diagonal = jnp.where(iota((rows, rows), 0) == iota((rows, rows), 1), 1.0, 0.0).astype(BF16)

    chip_sum(3)
    for i in range(2, 6):
        ring[i].wait_recv()
    acc[3] = acc[3] + fin_left[...] + fin_right[...]
    sum_high, sum_low = split_two(acc[3])
    both = lax.dot_general(
        send_one[...], jnp.concatenate([sum_high, sum_low], axis=0), NT, preferred_element_type=F32)
    sent[...] = (both[:, :BLOCK] + both[:, BLOCK:]).reshape(n_pair, PAD, BLOCK)[:, :slots]

    def pair_copy(i):
        to = (me_p + i) % n_pair
        return pltpu.make_async_remote_copy(
            src_ref=sent.at[to], dst_ref=came.at[me_p], send_sem=pair_send.at[i], recv_sem=pair_recv.at[i],
            device_id=(to, me_v), device_id_type=MESH)

    @pl.loop(1, n_pair)
    def _(i):
        pair_copy(i).start()

    def turn_copy(i):
        to = (me_v + i) % VIRT
        src = acc.at[3, pl.ds(pl.multiple_of(to * 16, 16), 16)]
        dst = turned.at[pl.ds(pl.multiple_of(me_v * 16, 16), 16)]
        return pltpu.make_async_remote_copy(
            src_ref=src, dst_ref=dst, send_sem=turn_send.at[i], recv_sem=turn_recv.at[i],
            device_id=(me_p, to), device_id_type=MESH)

    for i in range(1, VIRT):
        turn_copy(i).start()
    mine = pl.ds(pl.multiple_of(me_v * 16, 16), 16)
    turned[mine, :] = acc[3, mine, :]
    for i in range(1, VIRT):
        turn_copy(i).wait_recv()
    own_high, own_low = split_two(turned[...])
    own_pair = lax.dot_general(diagonal, jnp.concatenate([own_high, own_low], axis=0), NT, preferred_element_type=F32)
    own_ref[...] = lax.dot_general(own_pair.astype(BF16), own_lanes, NN, preferred_element_type=F32)

    @pl.loop(1, n_pair)
    def _(i):
        pair_copy(i).wait_recv()

    rest = jnp.zeros((n_pair, PAD - slots, BLOCK), F32)
    came_high, came_low = split_two(jnp.concatenate([came[...], rest], axis=1).reshape(n_slots, BLOCK))
    fetched = lax.dot_general(
        take_one[...], jnp.concatenate([came_high, came_low], axis=1), NN, preferred_element_type=F32)
    fetched_ref[...] = lax.dot_general(fetched.astype(BF16), mirror_lanes, NN, preferred_element_type=F32)

    for k in range(NX):
        chip_copy(k).wait_send()
    for copy in ring:
        copy.wait_send()
    for i in range(1, VIRT):
        turn_copy(i).wait_send()

    @pl.loop(1, n_pair)
    def _(i):
        pair_copy(i).wait_send()


def per_device(n_pair, slots, amplitudes, integrals, mask, slab, owner):
    rows, cs, width = amplitudes.shape
    dma = pltpu.SemaphoreType.DMA
    n_slots = n_pair * PAD
    half = BLOCK // 2
    own, fetched = pl.pallas_call(
        functools.partial(kernel, n_pair, slots),
        out_shape=[jax.ShapeDtypeStruct((rows, BLOCK), F32)] * 2,
        in_specs=[
            pl.BlockSpec(memory_space=pl.ANY),
            pl.BlockSpec(memory_space=pl.ANY),
            pl.BlockSpec(memory_space=pltpu.VMEM),
            pl.BlockSpec(memory_space=pltpu.SMEM),
            pl.BlockSpec(memory_space=pltpu.VMEM),
        ],
        out_specs=[pl.BlockSpec(memory_space=pltpu.VMEM)] * 2,
        scratch_shapes=[
            pltpu.VMEM((rows, cs, width), BF16),
            pltpu.VMEM((rows, cs * width), BF16),
            pltpu.VMEM((NX, 32, CORES * 4, cs, width), BF16),
            pltpu.VMEM((2, CORES * BLOCK, cs * width), BF16),
            pltpu.VMEM((NX, CORES, BLOCK, rows), F32),
            pltpu.VMEM((NX, BLOCK, rows), F32),
            pltpu.VMEM((NX, BLOCK, rows), F32),
            pltpu.VMEM((2, half, rows), F32),
            pltpu.VMEM((BLOCK, rows), F32),
            pltpu.VMEM((BLOCK, rows), F32),
            pltpu.VMEM((BLOCK, rows), F32),
            pltpu.VMEM((n_pair, slots, BLOCK), F32),
            pltpu.VMEM((n_pair, slots, BLOCK), F32),
            pltpu.VMEM((n_slots, rows), BF16),
            pltpu.VMEM((rows, n_slots), BF16),
            dma((rows // 128,)),
            dma((NX,)),
            dma((NX,)),
            dma((NX,)),
            dma((6,)),
            dma((6,)),
            dma((VIRT,)),
            dma((VIRT,)),
            dma((n_pair,)),
            dma((n_pair,)),
        ],
        compiler_params=pltpu.CompilerParams(
            collective_id=0, has_side_effects=True, vmem_limit_bytes=56 * 2**20),
        cost_estimate=pl.CostEstimate(
            flops=2 * rows * cs * width * VIRT * BLOCK, bytes_accessed=13 * 2**20, transcendentals=0),
    )(amplitudes, integrals.reshape(32, 32, cs, width), jnp.transpose(mask, (1, 2, 0)), slab, owner.reshape(-1, 128))
    return own + fetched


def solution(mesh, slots=17):
    return jax.shard_map(
        functools.partial(per_device, mesh.shape["pair"], slots),
        mesh=mesh,
        in_specs=(
            P("pair", None, "virt"),
            P(None, None, "virt"),
            P("pair", None, "virt"),
            P(),
            P(),
        ),
        out_specs=P("pair", "virt"),
        check_vma=False,
    )
```

```python
import functools

import jax
import jax.numpy as jnp
from jax import lax
from jax.experimental import pallas as pl
from jax.experimental.pallas import tpu as pltpu
from jax.sharding import PartitionSpec as P

MESH = pl.DeviceIdType.MESH
F32 = jnp.float32
BF16 = jnp.bfloat16
NX = 4
CORES = 2
VIRT = NX * CORES
BLOCK = 128
PAD = 24
NZ = 8
SPAN = 256
HALF = BLOCK // 2
GROUPS = 2
NT = (((1,), (1,)), ((), ()))
NN = (((1,), (0,)), ((), ()))


def split_two(value):
    high = value.astype(BF16)
    return high, (value - high.astype(F32)).astype(BF16)


def iota(shape, dim):
    return lax.broadcasted_iota(jnp.int32, shape, dim)


def flatten_into(dst, row, block, cs, width):
    flat = pltpu.einshape("pcd->p(cd)", block)
    for j in range(2):
        for c in range(cs):
            at = j * cs * 128 + c * 128
            dst[pl.ds(row, 16), at:at + 128] = flat[:, c * width + j * 128:c * width + (j + 1) * 128]


def kernel(
    n_pair, slots,
    amp, ints, mask, slab_ref, owner, out,
    amp_raw, amp_flat, int_raw, int_flat, part, chip_in, acc, fwd, fin_left, fin_right,
    turned, partial, sent, came, send_one, take_one, mask_ref, owner_ref, result,
    amp_sem, int_sem, small_sem, out_sem,
    chip_send, chip_recv, ring_send, ring_recv, turn_send, turn_recv, pair_send, pair_recv,
):
    rows, cs, width = amp_raw.shape
    tiles = rows // 128
    half_k = cs * 128
    spans = rows // SPAN
    me_p = lax.axis_index("pair")
    me_v = lax.axis_index("virt")
    x = me_v // CORES
    core = me_v % CORES
    other = me_v + 1 - 2 * core
    right = ((x + 1) % NX) * CORES + core
    left = ((x + NX - 1) % NX) * CORES + core

    def fetch_amp(q):
        at = pl.ds(q * 128, 128)
        return pltpu.make_async_copy(amp.at[at], amp_raw.at[at], amp_sem.at[q])

    def fetch_ints(s):
        to = (x + (2, 1, 3, 0)[s]) % NX
        return pltpu.make_async_copy(ints.at[:, pl.ds(to * CORES * 4, CORES * 4)], int_raw.at[s], int_sem.at[s])

    fetch_mask = pltpu.make_async_copy(mask, mask_ref, small_sem.at[0])
    fetch_owner = pltpu.make_async_copy(owner, owner_ref, small_sem.at[1])
    fetch_amp(0).start()
    fetch_amp(1).start()
    fetch_ints(0).start()
    fetch_mask.start()
    for q in range(2, tiles):
        fetch_amp(q).start()
    for s in range(1, NX):
        fetch_ints(s).start()
    fetch_owner.start()

    barrier = pltpu.get_barrier_semaphore()

    @pl.loop(1, VIRT)
    def _(i):
        pl.semaphore_signal(barrier, inc=1, device_id=(me_p, (me_v + i) % VIRT), device_id_type=MESH)

    @pl.loop(1, n_pair)
    def _(i):
        pl.semaphore_signal(barrier, inc=1, device_id=((me_p + i) % n_pair, me_v), device_id_type=MESH)

    def arrange_amp(q):
        fetch_amp(q).wait()

        @pl.loop(0, 8, unroll=4)
        def _(g):
            row = pl.multiple_of(q * 128 + g * 16, 16)
            flatten_into(amp_flat, row, amp_raw[pl.ds(row, 16)], cs, width)

    runs = (((0, 0), (0, 4)), ((1, 4), (2, 0)), ((1, 0), (2, 4)), ((3, 0), (3, 4)))

    def arrange(k):
        flat = int_flat.at[k % 2]
        for c in range(CORES):
            for r in range(2):
                s, first = runs[k][r]

                @pl.loop(0, 4, unroll=4)
                def _(g):
                    block = jnp.concatenate(
                        [int_raw[s, (first + g) * 4 + a, pl.ds(c * 4, 4)] for a in range(4)], axis=0)
                    row = pl.multiple_of((c * 8 + r * 4 + g) * 16, 16)
                    flatten_into(flat, row, block, cs, width)

    def multiply(k, nb):
        flat = int_flat.at[k % 2]
        ps = slice(nb * SPAN, (nb + 1) * SPAN)
        one = lax.dot_general(flat[:, :half_k], amp_flat[ps, :half_k], NT, preferred_element_type=F32)
        two = lax.dot_general(flat[:, half_k:], amp_flat[ps, half_k:], NT, preferred_element_type=F32)
        value = one * select[0:1, ps] + two * select[1:2, ps]
        for c in range(CORES):
            part[k, nb, c] = value[c * BLOCK:(c + 1) * BLOCK]
        if k == 0 and nb == 0:
            pl.semaphore_wait(barrier, VIRT - 1 + n_pair - 1)
        chip_copy(k, nb).start()

    def chip_copy(k, nb):
        return pltpu.make_async_remote_copy(
            src_ref=part.at[k, nb, 1 - core], dst_ref=chip_in.at[k, nb],
            send_sem=chip_send.at[k, nb], recv_sem=chip_recv.at[k, nb],
            device_id=(me_p, other), device_id_type=MESH)

    def ring_copy(i, nb, src, dst, to):
        return pltpu.make_async_remote_copy(
            src_ref=src, dst_ref=dst, send_sem=ring_send.at[i, nb], recv_sem=ring_recv.at[i, nb],
            device_id=(me_p, to), device_id_type=MESH)

    low, high = pl.ds(0, HALF), pl.ds(HALF, HALF)
    ring = [[
        ring_copy(0, nb, acc.at[0, nb, low], fwd.at[0, nb], right),
        ring_copy(1, nb, acc.at[0, nb, high], fwd.at[1, nb], left),
        ring_copy(2, nb, acc.at[1, nb, low], fin_left.at[nb, high], right),
        ring_copy(3, nb, acc.at[1, nb, high], fin_right.at[nb, low], left),
        ring_copy(4, nb, acc.at[2, nb, low], fin_left.at[nb, low], right),
        ring_copy(5, nb, acc.at[2, nb, high], fin_right.at[nb, high], left),
    ] for nb in range(spans)]

    def chip_sum(k, nb):
        chip_copy(k, nb).wait_recv()
        acc[k, nb] = part[k, nb, core] + chip_in[k, nb]

    def send_direct(k, nb):
        chip_sum(k, nb)
        ring[nb][2 * k].start()
        ring[nb][2 * k + 1].start()

    def send_forward(nb):
        chip_sum(2, nb)
        ring[nb][0].wait_recv()
        acc[2, nb, low] += fwd[0, nb]
        ring[nb][4].start()
        ring[nb][1].wait_recv()
        acc[2, nb, high] += fwd[1, nb]
        ring[nb][5].start()

    arrange_amp(0)
    arrange_amp(1)
    fetch_ints(0).wait()
    arrange(0)
    fetch_mask.wait()
    select = mask_ref[slab_ref[0] // 8].astype(F32)
    multiply(0, 0)
    arrange_amp(2)
    arrange_amp(3)
    multiply(0, 1)
    send_direct(0, 0)
    fetch_ints(1).wait()
    fetch_ints(2).wait()
    arrange(1)
    send_direct(0, 1)
    multiply(1, 0)
    multiply(1, 1)
    arrange(2)
    send_direct(1, 0)
    multiply(2, 0)
    send_direct(1, 1)
    multiply(2, 1)
    fetch_ints(3).wait()
    arrange(3)
    send_forward(0)
    multiply(3, 0)
    send_forward(1)
    multiply(3, 1)
    fetch_owner.wait()

    eye = iota((128, 128), 0) == iota((128, 128), 1)

    def as_column(row):
        return jnp.sum(jnp.where(eye, row, 0.0), axis=1, keepdims=True)

    def as_row(column):
        return jnp.sum(jnp.where(eye, column, 0.0), axis=0, keepdims=True)

    own_rows = [owner_ref[pl.ds(me_p * tiles + t, 1), :] for t in range(tiles)]
    wanted = [as_column((r ^ 1).astype(F32)).astype(jnp.int32) for r in own_rows]
    order_rows = [(r // 2).astype(F32) for r in own_rows]
    order_columns = [as_column(r) for r in order_rows]
    there_columns = []
    for t in range(tiles):
        want = jnp.broadcast_to(wanted[t], (128, 128))

        def look(g, found):
            return jnp.where(owner_ref[pl.ds(g, 1), :] == want, g // tiles, found)

        found = lax.fori_loop(0, n_pair * tiles, look, jnp.zeros((128, 128), jnp.int32), unroll=4)
        there_columns.append(jnp.max(found.astype(F32), axis=1, keepdims=True))
    there_rows = [as_row(c) for c in there_columns]

    steps = [(dy, dz) for dy in range(n_pair // NZ) for dz in range(NZ) if dy or dz]
    steps.sort(key=lambda s: (-min(s[0], n_pair // NZ - s[0]) - min(s[1], NZ - s[1]), s))
    me_y, me_z = me_p // NZ, me_p % NZ

    def number(code):
        found = jnp.zeros(code.shape, jnp.int32)
        for i, (dy, dz) in enumerate(steps):
            found = jnp.where(code == dy * NZ + dz, i, found)
        return found

    n_slots = n_pair * PAD
    for t in range(tiles):
        before = jnp.zeros((128, 128), F32)
        for u in range(tiles):
            hit = (there_rows[u] == there_columns[t]) & (order_rows[u] < order_columns[t])
            before = before + jnp.where(hit, 1.0, 0.0)
        rank = as_row(jnp.sum(before, axis=1, keepdims=True)).astype(jnp.int32)
        there = there_rows[t].astype(jnp.int32)
        y, z = there // NZ, there % NZ
        ahead = ((y - me_y + n_pair) % (n_pair // NZ)) * NZ + (z - me_z + NZ) % NZ
        behind = ((me_y - y + n_pair) % (n_pair // NZ)) * NZ + (me_z - z + NZ) % NZ
        at = slice(t * 128, (t + 1) * 128)
        row = number(ahead) * PAD + rank
        send_one[:, at] = jnp.where(iota((n_slots, 128), 0) == row, 1.0, 0.0).astype(BF16)
        column = as_column((number(behind) * PAD + rank).astype(F32)).astype(jnp.int32)
        take_one[at, :] = jnp.where(iota((128, n_slots), 1) == column, 1.0, 0.0).astype(BF16)

    came[n_pair - 1] = jnp.zeros((slots, BLOCK), F32)
    source, target = iota((BLOCK, BLOCK), 0), iota((BLOCK, BLOCK), 1)
    group, first, second = source // 16, (source // 4) % 4, source % 4
    own_lanes = jnp.where(target == first * 32 + group * 4 + second, 1.0, 0.0).astype(BF16)
    mirror_lanes = jnp.where(target == second * 32 + group * 4 + first, 1.0, 0.0).astype(BF16)
    own_lanes = jnp.concatenate([own_lanes, own_lanes], axis=0)
    mirror_lanes = jnp.concatenate([mirror_lanes, mirror_lanes], axis=0)
    diagonal = jnp.where(iota((SPAN, SPAN), 0) == iota((SPAN, SPAN), 1), 1.0, 0.0).astype(BF16)

    def finish(nb):
        chip_sum(3, nb)
        for i in range(2, 6):
            ring[nb][i].wait_recv()
        value = acc[3, nb] + fin_left[nb] + fin_right[nb]
        acc[3, nb] = value
        return jnp.concatenate(split_two(value), axis=0)

    def pair_copy(i):
        dy, dz = steps[i]
        to = ((me_y + dy) % (n_pair // NZ)) * NZ + (me_z + dz) % NZ
        return pltpu.make_async_remote_copy(
            src_ref=sent.at[i], dst_ref=came.at[i], send_sem=pair_send.at[i], recv_sem=pair_recv.at[i],
            device_id=(to, me_v), device_id_type=MESH)

    partial[...] = lax.dot_general(send_one[:, :SPAN], finish(0), NT, preferred_element_type=F32)
    rest = finish(1)
    eighth = n_pair // 4
    for g in range(4):
        at = slice(g * eighth * PAD, (g + 1) * eighth * PAD)
        both = partial[at, :] + lax.dot_general(send_one[at, SPAN:], rest, NT, preferred_element_type=F32)
        sent[g * eighth:(g + 1) * eighth] = (both[:, :BLOCK] + both[:, BLOCK:]).reshape(eighth, PAD, BLOCK)[:, :slots]
        for i in range(g * eighth, min((g + 1) * eighth, n_pair - 1)):
            pair_copy(i).start()

    def turn_copy(i):
        to = (me_v + i) % VIRT
        src = acc.at[3, :, pl.ds(pl.multiple_of(to * 16, 16), 16)]
        dst = turned.at[:, pl.ds(pl.multiple_of(me_v * 16, 16), 16)]
        return pltpu.make_async_remote_copy(
            src_ref=src, dst_ref=dst, send_sem=turn_send.at[i], recv_sem=turn_recv.at[i],
            device_id=(me_p, to), device_id_type=MESH)

    for i in range(1, VIRT):
        turn_copy(i).start()
    mine = pl.ds(pl.multiple_of(me_v * 16, 16), 16)
    for nb in range(spans):
        turned[nb, mine, :] = acc[3, nb, mine, :]
    for i in range(1, VIRT):
        turn_copy(i).wait_recv()
    for nb in range(spans):
        at = slice(nb * SPAN, (nb + 1) * SPAN)
        own = lax.dot_general(
            diagonal, jnp.concatenate(split_two(turned[nb]), axis=0), NT, preferred_element_type=F32)
        result[at, :] = lax.dot_general(own.astype(BF16), own_lanes, NN, preferred_element_type=F32)

    def out_copy(t):
        at = pl.ds(t * 128, 128)
        return pltpu.make_async_copy(result.at[at], out.at[at], out_sem.at[t])

    some = n_pair // GROUPS
    pad = jnp.zeros((some, PAD - slots, BLOCK), F32)
    for g in range(GROUPS):
        for i in range(g * some, min((g + 1) * some, n_pair - 1)):
            pair_copy(i).wait_recv()
        rows_in = jnp.concatenate([came[g * some:(g + 1) * some], pad], axis=1).reshape(some * PAD, BLOCK)
        rows_in = jnp.concatenate(split_two(rows_in), axis=1)
        for t in range(tiles):
            at = slice(t * 128, (t + 1) * 128)
            fetched = lax.dot_general(
                take_one[at, g * some * PAD:(g + 1) * some * PAD], rows_in, NN, preferred_element_type=F32)
            result[at, :] += lax.dot_general(fetched.astype(BF16), mirror_lanes, NN, preferred_element_type=F32)
            if g == GROUPS - 1:
                out_copy(t).start()
    for t in range(tiles):
        out_copy(t).wait()

    for nb in range(spans):
        for k in range(NX):
            chip_copy(k, nb).wait_send()
        for copy in ring[nb]:
            copy.wait_send()
    for i in range(1, VIRT):
        turn_copy(i).wait_send()
    for i in range(n_pair - 1):
        pair_copy(i).wait_send()


def per_device(n_pair, slots, amplitudes, integrals, mask, slab, owner):
    rows, cs, width = amplitudes.shape
    dma = pltpu.SemaphoreType.DMA
    n_slots = n_pair * PAD
    spans = rows // SPAN
    anywhere = pl.BlockSpec(memory_space=pl.ANY)
    return pl.pallas_call(
        functools.partial(kernel, n_pair, slots),
        out_shape=jax.ShapeDtypeStruct((rows, BLOCK), F32),
        in_specs=[anywhere, anywhere, anywhere, pl.BlockSpec(memory_space=pltpu.SMEM), anywhere],
        out_specs=anywhere,
        scratch_shapes=[
            pltpu.VMEM((rows, cs, width), BF16),
            pltpu.VMEM((rows, cs * width), BF16),
            pltpu.VMEM((NX, 32, CORES * 4, cs, width), BF16),
            pltpu.VMEM((2, CORES * BLOCK, cs * width), BF16),
            pltpu.VMEM((NX, spans, CORES, BLOCK, SPAN), F32),
            pltpu.VMEM((NX, spans, BLOCK, SPAN), F32),
            pltpu.VMEM((NX, spans, BLOCK, SPAN), F32),
            pltpu.VMEM((2, spans, HALF, SPAN), F32),
            pltpu.VMEM((spans, BLOCK, SPAN), F32),
            pltpu.VMEM((spans, BLOCK, SPAN), F32),
            pltpu.VMEM((spans, BLOCK, SPAN), F32),
            pltpu.VMEM((n_slots, 2 * BLOCK), F32),
            pltpu.VMEM((n_pair, slots, BLOCK), F32),
            pltpu.VMEM((n_pair, slots, BLOCK), F32),
            pltpu.VMEM((n_slots, rows), BF16),
            pltpu.VMEM((rows, n_slots), BF16),
            pltpu.VMEM((16, 2, rows), jnp.int32),
            pltpu.VMEM((n_pair * rows // 128, 128), jnp.int32),
            pltpu.VMEM((rows, BLOCK), F32),
            dma((rows // 128,)),
            dma((NX,)),
            dma((2,)),
            dma((rows // 128,)),
            dma((NX, spans)),
            dma((NX, spans)),
            dma((6, spans)),
            dma((6, spans)),
            dma((VIRT,)),
            dma((VIRT,)),
            dma((n_pair,)),
            dma((n_pair,)),
        ],
        compiler_params=pltpu.CompilerParams(
            collective_id=0, has_side_effects=True, vmem_limit_bytes=56 * 2**20),
        cost_estimate=pl.CostEstimate(
            flops=2 * rows * cs * width * VIRT * BLOCK, bytes_accessed=13 * 2**20, transcendentals=0),
    )(amplitudes, integrals.reshape(32, 32, cs, width), jnp.transpose(mask, (1, 2, 0)), slab, owner.reshape(-1, 128))


def solution(mesh, slots=17):
    return jax.shard_map(
        functools.partial(per_device, mesh.shape["pair"], slots),
        mesh=mesh,
        in_specs=(
            P("pair", None, "virt"),
            P(None, None, "virt"),
            P("pair", None, "virt"),
            P(),
            P(),
        ),
        out_specs=P("pair", "virt"),
        check_vma=False,
    )
```

```python
import functools

import jax
import jax.numpy as jnp
from jax import lax
from jax.experimental import pallas as pl
from jax.experimental.pallas import tpu as pltpu
from jax.sharding import PartitionSpec as P

MESH = pl.DeviceIdType.MESH
F32 = jnp.float32
BF16 = jnp.bfloat16
NX = 4
CORES = 2
VIRT = NX * CORES
BLOCK = 128
PAD = 24
NZ = 8
SPAN = 256
HALF = BLOCK // 2
GROUPS = 2
NT = (((1,), (1,)), ((), ()))
NN = (((1,), (0,)), ((), ()))


def split_two(value):
    high = value.astype(BF16)
    return high, (value - high.astype(F32)).astype(BF16)


def iota(shape, dim):
    return lax.broadcasted_iota(jnp.int32, shape, dim)


def flatten_into(dst, row, block, cs, width):
    flat = pltpu.einshape("pcd->p(cd)", block)
    for j in range(2):
        for c in range(cs):
            at = j * cs * 128 + c * 128
            dst[pl.ds(row, 16), at:at + 128] = flat[:, c * width + j * 128:c * width + (j + 1) * 128]


def kernel(
    n_pair, slots,
    amp, ints, mask, slab_ref, owner, out,
    amp_raw, amp_flat, int_raw, int_flat, part, chip_in, acc, fwd, fin_left, fin_right,
    turned, partial, sent, came, send_one, take_one, mask_ref, owner_ref, result, looks,
    amp_sem, int_sem, small_sem, out_sem,
    chip_send, chip_recv, ring_send, ring_recv, turn_send, turn_recv, pair_send, pair_recv, look_send, look_recv,
):
    rows, cs, width = amp_raw.shape
    tiles = rows // 128
    half_k = cs * 128
    spans = rows // SPAN
    me_p = lax.axis_index("pair")
    me_v = lax.axis_index("virt")
    x = me_v // CORES
    core = me_v % CORES
    other = me_v + 1 - 2 * core
    right = ((x + 1) % NX) * CORES + core
    left = ((x + NX - 1) % NX) * CORES + core

    def fetch_amp(q):
        at = pl.ds(q * 128, 128)
        return pltpu.make_async_copy(amp.at[at], amp_raw.at[at], amp_sem.at[q])

    def fetch_ints(s):
        to = (x + (2, 1, 3, 0)[s]) % NX
        return pltpu.make_async_copy(ints.at[:, pl.ds(to * CORES * 4, CORES * 4)], int_raw.at[s], int_sem.at[s])

    fetch_mask = pltpu.make_async_copy(mask, mask_ref, small_sem.at[0])
    fetch_owner = pltpu.make_async_copy(owner, owner_ref, small_sem.at[1])
    fetch_amp(0).start()
    fetch_amp(1).start()
    fetch_ints(0).start()
    fetch_mask.start()
    for q in range(2, tiles):
        fetch_amp(q).start()
    for s in range(1, NX):
        fetch_ints(s).start()
    fetch_owner.start()

    barrier = pltpu.get_barrier_semaphore()

    @pl.loop(1, VIRT)
    def _(i):
        pl.semaphore_signal(barrier, inc=1, device_id=(me_p, (me_v + i) % VIRT), device_id_type=MESH)

    @pl.loop(1, n_pair)
    def _(i):
        pl.semaphore_signal(barrier, inc=1, device_id=((me_p + i) % n_pair, me_v), device_id_type=MESH)

    def arrange_amp(q):
        fetch_amp(q).wait()

        @pl.loop(0, 8, unroll=4)
        def _(g):
            row = pl.multiple_of(q * 128 + g * 16, 16)
            flatten_into(amp_flat, row, amp_raw[pl.ds(row, 16)], cs, width)

    runs = (((0, 0), (0, 4)), ((1, 4), (2, 0)), ((1, 0), (2, 4)), ((3, 0), (3, 4)))

    def arrange(k):
        flat = int_flat.at[k % 2]
        for c in range(CORES):
            for r in range(2):
                s, first = runs[k][r]

                @pl.loop(0, 4, unroll=4)
                def _(g):
                    block = jnp.concatenate(
                        [int_raw[s, (first + g) * 4 + a, pl.ds(c * 4, 4)] for a in range(4)], axis=0)
                    row = pl.multiple_of((c * 8 + r * 4 + g) * 16, 16)
                    flatten_into(flat, row, block, cs, width)

    def multiply(k, nb):
        flat = int_flat.at[k % 2]
        ps = slice(nb * SPAN, (nb + 1) * SPAN)
        one = lax.dot_general(flat[:, :half_k], amp_flat[ps, :half_k], NT, preferred_element_type=F32)
        two = lax.dot_general(flat[:, half_k:], amp_flat[ps, half_k:], NT, preferred_element_type=F32)
        value = one * select[0:1, ps] + two * select[1:2, ps]
        for c in range(CORES):
            part[k, nb, c] = value[c * BLOCK:(c + 1) * BLOCK]
        if k == 0 and nb == 0:
            pl.semaphore_wait(barrier, VIRT - 1 + n_pair - 1)
        chip_copy(k, nb).start()

    def chip_copy(k, nb):
        return pltpu.make_async_remote_copy(
            src_ref=part.at[k, nb, 1 - core], dst_ref=chip_in.at[k, nb],
            send_sem=chip_send.at[k, nb], recv_sem=chip_recv.at[k, nb],
            device_id=(me_p, other), device_id_type=MESH)

    def ring_copy(i, nb, src, dst, to):
        return pltpu.make_async_remote_copy(
            src_ref=src, dst_ref=dst, send_sem=ring_send.at[i, nb], recv_sem=ring_recv.at[i, nb],
            device_id=(me_p, to), device_id_type=MESH)

    low, high = pl.ds(0, HALF), pl.ds(HALF, HALF)
    ring = [[
        ring_copy(0, nb, acc.at[0, nb, low], fwd.at[0, nb], right),
        ring_copy(1, nb, acc.at[0, nb, high], fwd.at[1, nb], left),
        ring_copy(2, nb, acc.at[1, nb, low], fin_left.at[nb, high], right),
        ring_copy(3, nb, acc.at[1, nb, high], fin_right.at[nb, low], left),
        ring_copy(4, nb, acc.at[2, nb, low], fin_left.at[nb, low], right),
        ring_copy(5, nb, acc.at[2, nb, high], fin_right.at[nb, high], left),
    ] for nb in range(spans)]

    def chip_sum(k, nb):
        chip_copy(k, nb).wait_recv()
        acc[k, nb] = part[k, nb, core] + chip_in[k, nb]

    def send_direct(k, nb):
        chip_sum(k, nb)
        ring[nb][2 * k].start()
        ring[nb][2 * k + 1].start()

    def send_forward(nb):
        chip_sum(2, nb)
        ring[nb][0].wait_recv()
        acc[2, nb, low] += fwd[0, nb]
        ring[nb][4].start()
        ring[nb][1].wait_recv()
        acc[2, nb, high] += fwd[1, nb]
        ring[nb][5].start()

    eye = iota((128, 128), 0) == iota((128, 128), 1)

    def as_column(row):
        return jnp.sum(jnp.where(eye, row, 0.0), axis=1, keepdims=True)

    def as_row(column):
        return jnp.sum(jnp.where(eye, column, 0.0), axis=0, keepdims=True)

    def look_copy(i):
        return pltpu.make_async_remote_copy(
            src_ref=looks.at[me_v], dst_ref=looks.at[me_v], send_sem=look_send.at[i], recv_sem=look_recv.at[i],
            device_id=(me_p, (me_v + i) % VIRT), device_id_type=MESH)

    share = n_pair * tiles // VIRT

    def search():
        fetch_owner.wait()
        found_rows = []
        for t in range(tiles):
            row = owner_ref[pl.ds(me_p * tiles + t, 1), :]
            want = jnp.broadcast_to(as_column((row ^ 1).astype(F32)).astype(jnp.int32), (128, 128))

            def look(i, found):
                g = me_v * share + i
                return jnp.where(owner_ref[pl.ds(g, 1), :] == want, g // tiles, found)

            found = lax.fori_loop(0, share, look, jnp.zeros((128, 128), jnp.int32), unroll=4)
            found_rows.append(as_row(jnp.max(found.astype(F32), axis=1, keepdims=True)))
        looks[me_v] = jnp.concatenate(found_rows + [jnp.zeros((8 - tiles, 128), F32)], axis=0)
        for i in range(1, VIRT):
            look_copy(i).start()

    arrange_amp(0)
    arrange_amp(1)
    fetch_ints(0).wait()
    arrange(0)
    fetch_mask.wait()
    select = mask_ref[slab_ref[0] // 8].astype(F32)
    multiply(0, 0)
    arrange_amp(2)
    arrange_amp(3)
    multiply(0, 1)
    send_direct(0, 0)
    fetch_ints(1).wait()
    fetch_ints(2).wait()
    arrange(1)
    send_direct(0, 1)
    multiply(1, 0)
    multiply(1, 1)
    arrange(2)
    send_direct(1, 0)
    multiply(2, 0)
    send_direct(1, 1)
    search()
    multiply(2, 1)
    fetch_ints(3).wait()
    arrange(3)
    send_forward(0)
    multiply(3, 0)
    send_forward(1)
    multiply(3, 1)

    for i in range(1, VIRT):
        look_copy(i).wait_recv()
    there_all = looks[0]
    for v in range(1, VIRT):
        there_all = there_all + looks[v]
    there_rows = [there_all[t:t + 1] for t in range(tiles)]
    there_columns = [as_column(r) for r in there_rows]
    order_rows = [(owner_ref[pl.ds(me_p * tiles + t, 1), :] // 2).astype(F32) for t in range(tiles)]
    order_columns = [as_column(r) for r in order_rows]


    steps = [(dy, dz) for dy in range(n_pair // NZ) for dz in range(NZ) if dy or dz]
    steps.sort(key=lambda s: (-min(s[0], n_pair // NZ - s[0]) - min(s[1], NZ - s[1]), s))
    me_y, me_z = me_p // NZ, me_p % NZ

    def number(code):
        found = jnp.zeros(code.shape, jnp.int32)
        for i, (dy, dz) in enumerate(steps):
            found = jnp.where(code == dy * NZ + dz, i, found)
        return found

    n_slots = n_pair * PAD
    for t in range(tiles):
        before = jnp.zeros((128, 128), F32)
        for u in range(tiles):
            hit = (there_rows[u] == there_columns[t]) & (order_rows[u] < order_columns[t])
            before = before + jnp.where(hit, 1.0, 0.0)
        rank = as_row(jnp.sum(before, axis=1, keepdims=True)).astype(jnp.int32)
        there = there_rows[t].astype(jnp.int32)
        y, z = there // NZ, there % NZ
        ahead = ((y - me_y + n_pair) % (n_pair // NZ)) * NZ + (z - me_z + NZ) % NZ
        behind = ((me_y - y + n_pair) % (n_pair // NZ)) * NZ + (me_z - z + NZ) % NZ
        at = slice(t * 128, (t + 1) * 128)
        row = number(ahead) * PAD + rank
        send_one[:, at] = jnp.where(iota((n_slots, 128), 0) == row, 1.0, 0.0).astype(BF16)
        column = as_column((number(behind) * PAD + rank).astype(F32)).astype(jnp.int32)
        take_one[at, :] = jnp.where(iota((128, n_slots), 1) == column, 1.0, 0.0).astype(BF16)

    came[n_pair - 1] = jnp.zeros((slots, BLOCK), F32)
    source, target = iota((BLOCK, BLOCK), 0), iota((BLOCK, BLOCK), 1)
    group, first, second = source // 16, (source // 4) % 4, source % 4
    own_lanes = jnp.where(target == first * 32 + group * 4 + second, 1.0, 0.0).astype(BF16)
    mirror_lanes = jnp.where(target == second * 32 + group * 4 + first, 1.0, 0.0).astype(BF16)
    own_lanes = jnp.concatenate([own_lanes, own_lanes], axis=0)
    mirror_lanes = jnp.concatenate([mirror_lanes, mirror_lanes], axis=0)
    diagonal = jnp.where(iota((SPAN, SPAN), 0) == iota((SPAN, SPAN), 1), 1.0, 0.0).astype(BF16)

    def finish(nb):
        chip_sum(3, nb)
        for i in range(2, 6):
            ring[nb][i].wait_recv()
        value = acc[3, nb] + fin_left[nb] + fin_right[nb]
        acc[3, nb] = value
        return jnp.concatenate(split_two(value), axis=0)

    def pair_copy(i):
        dy, dz = steps[i]
        to = ((me_y + dy) % (n_pair // NZ)) * NZ + (me_z + dz) % NZ
        return pltpu.make_async_remote_copy(
            src_ref=sent.at[i], dst_ref=came.at[i], send_sem=pair_send.at[i], recv_sem=pair_recv.at[i],
            device_id=(to, me_v), device_id_type=MESH)

    partial[...] = lax.dot_general(send_one[:, :SPAN], finish(0), NT, preferred_element_type=F32)
    rest = finish(1)
    eighth = n_pair // 4
    for g in range(4):
        at = slice(g * eighth * PAD, (g + 1) * eighth * PAD)
        both = partial[at, :] + lax.dot_general(send_one[at, SPAN:], rest, NT, preferred_element_type=F32)
        sent[g * eighth:(g + 1) * eighth] = (both[:, :BLOCK] + both[:, BLOCK:]).reshape(eighth, PAD, BLOCK)[:, :slots]
        for i in range(g * eighth, min((g + 1) * eighth, n_pair - 1)):
            pair_copy(i).start()

    def turn_copy(i):
        to = (me_v + i) % VIRT
        src = acc.at[3, :, pl.ds(pl.multiple_of(to * 16, 16), 16)]
        dst = turned.at[:, pl.ds(pl.multiple_of(me_v * 16, 16), 16)]
        return pltpu.make_async_remote_copy(
            src_ref=src, dst_ref=dst, send_sem=turn_send.at[i], recv_sem=turn_recv.at[i],
            device_id=(me_p, to), device_id_type=MESH)

    for i in range(1, VIRT):
        turn_copy(i).start()
    mine = pl.ds(pl.multiple_of(me_v * 16, 16), 16)
    for nb in range(spans):
        turned[nb, mine, :] = acc[3, nb, mine, :]
    for i in range(1, VIRT):
        turn_copy(i).wait_recv()
    for nb in range(spans):
        at = slice(nb * SPAN, (nb + 1) * SPAN)
        own = lax.dot_general(
            diagonal, jnp.concatenate(split_two(turned[nb]), axis=0), NT, preferred_element_type=F32)
        result[at, :] = lax.dot_general(own.astype(BF16), own_lanes, NN, preferred_element_type=F32)

    def out_copy(t):
        at = pl.ds(t * 128, 128)
        return pltpu.make_async_copy(result.at[at], out.at[at], out_sem.at[t])

    for nb in range(spans):
        for k in range(NX):
            chip_copy(k, nb).wait_send()
        for copy in ring[nb]:
            copy.wait_send()
    for i in range(1, VIRT):
        turn_copy(i).wait_send()
        look_copy(i).wait_send()

    some = n_pair // GROUPS
    pad = jnp.zeros((some, PAD - slots, BLOCK), F32)
    for g in range(GROUPS):
        for i in range(g * some, min((g + 1) * some, n_pair - 1)):
            pair_copy(i).wait_recv()
        rows_in = jnp.concatenate([came[g * some:(g + 1) * some], pad], axis=1).reshape(some * PAD, BLOCK)
        rows_in = jnp.concatenate(split_two(rows_in), axis=1)
        for t in range(tiles):
            at = slice(t * 128, (t + 1) * 128)
            fetched = lax.dot_general(
                take_one[at, g * some * PAD:(g + 1) * some * PAD], rows_in, NN, preferred_element_type=F32)
            result[at, :] += lax.dot_general(fetched.astype(BF16), mirror_lanes, NN, preferred_element_type=F32)
            if g == GROUPS - 1:
                out_copy(t).start()
    for i in range(n_pair - 1):
        pair_copy(i).wait_send()
    for t in range(tiles):
        out_copy(t).wait()


def per_device(n_pair, slots, amplitudes, integrals, mask, slab, owner):
    rows, cs, width = amplitudes.shape
    dma = pltpu.SemaphoreType.DMA
    n_slots = n_pair * PAD
    spans = rows // SPAN
    anywhere = pl.BlockSpec(memory_space=pl.ANY)
    return pl.pallas_call(
        functools.partial(kernel, n_pair, slots),
        out_shape=jax.ShapeDtypeStruct((rows, BLOCK), F32),
        in_specs=[anywhere, anywhere, anywhere, pl.BlockSpec(memory_space=pltpu.SMEM), anywhere],
        out_specs=anywhere,
        scratch_shapes=[
            pltpu.VMEM((rows, cs, width), BF16),
            pltpu.VMEM((rows, cs * width), BF16),
            pltpu.VMEM((NX, 32, CORES * 4, cs, width), BF16),
            pltpu.VMEM((2, CORES * BLOCK, cs * width), BF16),
            pltpu.VMEM((NX, spans, CORES, BLOCK, SPAN), F32),
            pltpu.VMEM((NX, spans, BLOCK, SPAN), F32),
            pltpu.VMEM((NX, spans, BLOCK, SPAN), F32),
            pltpu.VMEM((2, spans, HALF, SPAN), F32),
            pltpu.VMEM((spans, BLOCK, SPAN), F32),
            pltpu.VMEM((spans, BLOCK, SPAN), F32),
            pltpu.VMEM((spans, BLOCK, SPAN), F32),
            pltpu.VMEM((n_slots, 2 * BLOCK), F32),
            pltpu.VMEM((n_pair, slots, BLOCK), F32),
            pltpu.VMEM((n_pair, slots, BLOCK), F32),
            pltpu.VMEM((n_slots, rows), BF16),
            pltpu.VMEM((rows, n_slots), BF16),
            pltpu.VMEM((16, 2, rows), jnp.int32),
            pltpu.VMEM((n_pair * rows // 128, 128), jnp.int32),
            pltpu.VMEM((rows, BLOCK), F32),
            pltpu.VMEM((VIRT, 8, 128), F32),
            dma((rows // 128,)),
            dma((NX,)),
            dma((2,)),
            dma((rows // 128,)),
            dma((NX, spans)),
            dma((NX, spans)),
            dma((6, spans)),
            dma((6, spans)),
            dma((VIRT,)),
            dma((VIRT,)),
            dma((n_pair,)),
            dma((n_pair,)),
            dma((VIRT,)),
            dma((VIRT,)),
        ],
        compiler_params=pltpu.CompilerParams(
            collective_id=0, has_side_effects=True, vmem_limit_bytes=56 * 2**20),
        cost_estimate=pl.CostEstimate(
            flops=2 * rows * cs * width * VIRT * BLOCK, bytes_accessed=13 * 2**20, transcendentals=0),
    )(amplitudes, integrals.reshape(32, 32, cs, width), jnp.transpose(mask, (1, 2, 0)), slab, owner.reshape(-1, 128))


def solution(mesh, slots=17):
    return jax.shard_map(
        functools.partial(per_device, mesh.shape["pair"], slots),
        mesh=mesh,
        in_specs=(
            P("pair", None, "virt"),
            P(None, None, "virt"),
            P("pair", None, "virt"),
            P(),
            P(),
        ),
        out_specs=P("pair", "virt"),
        check_vma=False,
    )
```

```python
import functools

import jax
import jax.numpy as jnp
from jax import lax
from jax.experimental import pallas as pl
from jax.experimental.pallas import tpu as pltpu
from jax.sharding import PartitionSpec as P

MESH = pl.DeviceIdType.MESH
F32 = jnp.float32
BF16 = jnp.bfloat16
NX = 4
CORES = 2
VIRT = NX * CORES
BLOCK = 128
PAD = 24
NZ = 8
SPAN = 256
HALF = BLOCK // 2
GROUPS = 2
NT = (((1,), (1,)), ((), ()))
NN = (((1,), (0,)), ((), ()))


def split_two(value):
    high = value.astype(BF16)
    return high, (value - high.astype(F32)).astype(BF16)


def iota(shape, dim):
    return lax.broadcasted_iota(jnp.int32, shape, dim)


def flatten_into(dst, row, block, cs, width):
    flat = pltpu.einshape("pcd->p(cd)", block)
    for j in range(2):
        for c in range(cs):
            at = j * cs * 128 + c * 128
            dst[pl.ds(row, 16), at:at + 128] = flat[:, c * width + j * 128:c * width + (j + 1) * 128]


def kernel(
    n_pair, slots,
    amp, ints, mask, slab_ref, owner, out,
    amp_raw, amp_flat, int_raw, int_flat, part, chip_in, acc, fwd, fin_left, fin_right,
    turned, partial, sent, came, send_one, take_one, mask_ref, owner_ref, result, looks,
    amp_sem, int_sem, small_sem, out_sem,
    chip_send, chip_recv, ring_send, ring_recv, turn_send, turn_recv, pair_send, pair_recv, look_send, look_recv,
):
    rows, cs, width = amp_raw.shape
    tiles = rows // 128
    half_k = cs * 128
    spans = rows // SPAN
    me_p = lax.axis_index("pair")
    me_v = lax.axis_index("virt")
    x = me_v // CORES
    core = me_v % CORES
    other = me_v + 1 - 2 * core
    right = ((x + 1) % NX) * CORES + core
    left = ((x + NX - 1) % NX) * CORES + core

    def fetch_amp(q):
        at = pl.ds(q * 128, 128)
        return pltpu.make_async_copy(amp.at[at], amp_raw.at[at], amp_sem.at[q])

    def fetch_ints(s):
        to = (x + (2, 1, 3, 0)[s]) % NX
        return pltpu.make_async_copy(ints.at[:, pl.ds(to * CORES * 4, CORES * 4)], int_raw.at[s], int_sem.at[s])

    fetch_mask = pltpu.make_async_copy(mask, mask_ref, small_sem.at[0])
    fetch_owner = pltpu.make_async_copy(owner, owner_ref, small_sem.at[1])
    fetch_amp(0).start()
    fetch_amp(1).start()
    fetch_ints(0).start()
    fetch_mask.start()
    for q in range(2, tiles):
        fetch_amp(q).start()
    for s in range(1, NX):
        fetch_ints(s).start()
    fetch_owner.start()

    barrier = pltpu.get_barrier_semaphore()

    @pl.loop(1, VIRT)
    def _(i):
        pl.semaphore_signal(barrier, inc=1, device_id=(me_p, (me_v + i) % VIRT), device_id_type=MESH)

    @pl.loop(1, n_pair)
    def _(i):
        pl.semaphore_signal(barrier, inc=1, device_id=((me_p + i) % n_pair, me_v), device_id_type=MESH)

    def arrange_amp(q):
        fetch_amp(q).wait()

        @pl.loop(0, 8, unroll=4)
        def _(g):
            row = pl.multiple_of(q * 128 + g * 16, 16)
            flatten_into(amp_flat, row, amp_raw[pl.ds(row, 16)], cs, width)

    runs = (((0, 0), (0, 4)), ((1, 4), (2, 0)), ((1, 0), (2, 4)), ((3, 0), (3, 4)))

    def arrange(k):
        flat = int_flat.at[k % 2]
        for c in range(CORES):
            for r in range(2):
                s, first = runs[k][r]

                @pl.loop(0, 4, unroll=4)
                def _(g):
                    block = jnp.concatenate(
                        [int_raw[s, (first + g) * 4 + a, pl.ds(c * 4, 4)] for a in range(4)], axis=0)
                    row = pl.multiple_of((c * 8 + r * 4 + g) * 16, 16)
                    flatten_into(flat, row, block, cs, width)

    def multiply(k, nb):
        flat = int_flat.at[k % 2]
        ps = slice(nb * SPAN, (nb + 1) * SPAN)
        one = lax.dot_general(flat[:, :half_k], amp_flat[ps, :half_k], NT, preferred_element_type=F32)
        two = lax.dot_general(flat[:, half_k:], amp_flat[ps, half_k:], NT, preferred_element_type=F32)
        value = one * select[0:1, ps] + two * select[1:2, ps]
        for c in range(CORES):
            part[k, nb, c] = value[c * BLOCK:(c + 1) * BLOCK]
        if k == 0:
            if nb == 0:
                pl.semaphore_wait(barrier, VIRT - 1 + n_pair - 1)
            chip_copy(k, pl.ds(nb, 1), nb).start()
        elif nb == spans - 1:
            chip_copy(k, pl.ds(0, spans), 0).start()

    def chip_copy(k, at, i):
        return pltpu.make_async_remote_copy(
            src_ref=part.at[k, at, 1 - core], dst_ref=chip_in.at[k, at],
            send_sem=chip_send.at[k, i], recv_sem=chip_recv.at[k, i],
            device_id=(me_p, other), device_id_type=MESH)

    every = pl.ds(0, spans)
    chip_copies = [chip_copy(0, pl.ds(nb, 1), nb) for nb in range(spans)] + [chip_copy(k, every, 0) for k in range(1, NX)]

    def ring_copy(i, nb, src, dst, to):
        return pltpu.make_async_remote_copy(
            src_ref=src, dst_ref=dst, send_sem=ring_send.at[i, nb], recv_sem=ring_recv.at[i, nb],
            device_id=(me_p, to), device_id_type=MESH)

    low, high = pl.ds(0, HALF), pl.ds(HALF, HALF)
    starts = [(
        ring_copy(0, nb, acc.at[0, nb, low], fwd.at[0, nb], right),
        ring_copy(1, nb, acc.at[0, nb, high], fwd.at[1, nb], left),
    ) for nb in range(spans)]
    direct = (
        ring_copy(2, 0, acc.at[1, every, low], fin_left.at[every, high], right),
        ring_copy(3, 0, acc.at[1, every, high], fin_right.at[every, low], left),
    )
    forward = (
        ring_copy(4, 0, acc.at[2, every, low], fin_left.at[every, low], right),
        ring_copy(5, 0, acc.at[2, every, high], fin_right.at[every, high], left),
    )

    def send_start(nb):
        chip_copies[nb].wait_recv()
        acc[0, nb] = part[0, nb, core] + chip_in[0, nb]
        for copy in starts[nb]:
            copy.start()

    def chip_sum(k):
        chip_copies[spans + k - 1].wait_recv()
        for nb in range(spans):
            acc[k, nb] = part[k, nb, core] + chip_in[k, nb]

    def send_direct():
        chip_sum(1)
        for copy in direct:
            copy.start()

    def send_forward():
        chip_sum(2)
        for side, piece in enumerate((low, high)):
            for nb in range(spans):
                starts[nb][side].wait_recv()
                acc[2, nb, piece] += fwd[side, nb]
            forward[side].start()

    eye = iota((128, 128), 0) == iota((128, 128), 1)

    def as_column(row):
        return jnp.sum(jnp.where(eye, row, 0.0), axis=1, keepdims=True)

    def as_row(column):
        return jnp.sum(jnp.where(eye, column, 0.0), axis=0, keepdims=True)

    def look_copy(i):
        return pltpu.make_async_remote_copy(
            src_ref=looks.at[me_v], dst_ref=looks.at[me_v], send_sem=look_send.at[i], recv_sem=look_recv.at[i],
            device_id=(me_p, (me_v + i) % VIRT), device_id_type=MESH)

    share = n_pair * tiles // VIRT

    def search():
        fetch_owner.wait()
        found_rows = []
        for t in range(tiles):
            row = owner_ref[pl.ds(me_p * tiles + t, 1), :]
            want = jnp.broadcast_to(as_column((row ^ 1).astype(F32)).astype(jnp.int32), (128, 128))

            def look(i, found):
                g = me_v * share + i
                return jnp.where(owner_ref[pl.ds(g, 1), :] == want, g // tiles, found)

            found = lax.fori_loop(0, share, look, jnp.zeros((128, 128), jnp.int32), unroll=4)
            found_rows.append(as_row(jnp.max(found.astype(F32), axis=1, keepdims=True)))
        looks[me_v] = jnp.concatenate(found_rows + [jnp.zeros((8 - tiles, 128), F32)], axis=0)
        for i in range(1, VIRT):
            look_copy(i).start()

    arrange_amp(0)
    arrange_amp(1)
    fetch_ints(0).wait()
    arrange(0)
    fetch_mask.wait()
    select = mask_ref[slab_ref[0] // 8].astype(F32)
    multiply(0, 0)
    arrange_amp(2)
    arrange_amp(3)
    multiply(0, 1)
    send_start(0)
    fetch_ints(1).wait()
    fetch_ints(2).wait()
    arrange(1)
    send_start(1)
    multiply(1, 0)
    multiply(1, 1)
    arrange(2)
    send_direct()
    multiply(2, 0)
    search()
    multiply(2, 1)
    fetch_ints(3).wait()
    arrange(3)
    multiply(3, 0)
    send_forward()
    multiply(3, 1)

    for i in range(1, VIRT):
        look_copy(i).wait_recv()
    there_all = looks[0]
    for v in range(1, VIRT):
        there_all = there_all + looks[v]
    there_rows = [there_all[t:t + 1] for t in range(tiles)]
    there_columns = [as_column(r) for r in there_rows]
    order_rows = [(owner_ref[pl.ds(me_p * tiles + t, 1), :] // 2).astype(F32) for t in range(tiles)]
    order_columns = [as_column(r) for r in order_rows]


    steps = [(dy, dz) for dy in range(n_pair // NZ) for dz in range(NZ) if dy or dz]
    steps.sort(key=lambda s: (-min(s[0], n_pair // NZ - s[0]) - min(s[1], NZ - s[1]), s))
    me_y, me_z = me_p // NZ, me_p % NZ

    def number(code):
        found = jnp.zeros(code.shape, jnp.int32)
        for i, (dy, dz) in enumerate(steps):
            found = jnp.where(code == dy * NZ + dz, i, found)
        return found

    n_slots = n_pair * PAD
    for t in range(tiles):
        before = jnp.zeros((128, 128), F32)
        for u in range(tiles):
            hit = (there_rows[u] == there_columns[t]) & (order_rows[u] < order_columns[t])
            before = before + jnp.where(hit, 1.0, 0.0)
        rank = as_row(jnp.sum(before, axis=1, keepdims=True)).astype(jnp.int32)
        there = there_rows[t].astype(jnp.int32)
        y, z = there // NZ, there % NZ
        ahead = ((y - me_y + n_pair) % (n_pair // NZ)) * NZ + (z - me_z + NZ) % NZ
        behind = ((me_y - y + n_pair) % (n_pair // NZ)) * NZ + (me_z - z + NZ) % NZ
        at = slice(t * 128, (t + 1) * 128)
        row = number(ahead) * PAD + rank
        send_one[:, at] = jnp.where(iota((n_slots, 128), 0) == row, 1.0, 0.0).astype(BF16)
        column = as_column((number(behind) * PAD + rank).astype(F32)).astype(jnp.int32)
        take_one[at, :] = jnp.where(iota((128, n_slots), 1) == column, 1.0, 0.0).astype(BF16)

    came[n_pair - 1] = jnp.zeros((slots, BLOCK), F32)
    source, target = iota((BLOCK, BLOCK), 0), iota((BLOCK, BLOCK), 1)
    group, first, second = source // 16, (source // 4) % 4, source % 4
    own_lanes = jnp.where(target == first * 32 + group * 4 + second, 1.0, 0.0).astype(BF16)
    mirror_lanes = jnp.where(target == second * 32 + group * 4 + first, 1.0, 0.0).astype(BF16)
    own_lanes = jnp.concatenate([own_lanes, own_lanes], axis=0)
    mirror_lanes = jnp.concatenate([mirror_lanes, mirror_lanes], axis=0)
    diagonal = jnp.where(iota((SPAN, SPAN), 0) == iota((SPAN, SPAN), 1), 1.0, 0.0).astype(BF16)

    def finish(nb):
        if nb == 0:
            chip_sum(3)
            for copy in direct + forward:
                copy.wait_recv()
        value = acc[3, nb] + fin_left[nb] + fin_right[nb]
        acc[3, nb] = value
        return jnp.concatenate(split_two(value), axis=0)

    def pair_copy(i):
        dy, dz = steps[i]
        to = ((me_y + dy) % (n_pair // NZ)) * NZ + (me_z + dz) % NZ
        return pltpu.make_async_remote_copy(
            src_ref=sent.at[i], dst_ref=came.at[i], send_sem=pair_send.at[i], recv_sem=pair_recv.at[i],
            device_id=(to, me_v), device_id_type=MESH)

    partial[...] = lax.dot_general(send_one[:, :SPAN], finish(0), NT, preferred_element_type=F32)
    rest = finish(1)
    eighth = n_pair // 4
    for g in range(4):
        at = slice(g * eighth * PAD, (g + 1) * eighth * PAD)
        both = partial[at, :] + lax.dot_general(send_one[at, SPAN:], rest, NT, preferred_element_type=F32)
        sent[g * eighth:(g + 1) * eighth] = (both[:, :BLOCK] + both[:, BLOCK:]).reshape(eighth, PAD, BLOCK)[:, :slots]
        for i in range(g * eighth, min((g + 1) * eighth, n_pair - 1)):
            pair_copy(i).start()

    def turn_copy(i):
        to = (me_v + i) % VIRT
        src = acc.at[3, :, pl.ds(pl.multiple_of(to * 16, 16), 16)]
        dst = turned.at[:, pl.ds(pl.multiple_of(me_v * 16, 16), 16)]
        return pltpu.make_async_remote_copy(
            src_ref=src, dst_ref=dst, send_sem=turn_send.at[i], recv_sem=turn_recv.at[i],
            device_id=(me_p, to), device_id_type=MESH)

    for i in range(1, VIRT):
        turn_copy(i).start()
    mine = pl.ds(pl.multiple_of(me_v * 16, 16), 16)
    for nb in range(spans):
        turned[nb, mine, :] = acc[3, nb, mine, :]
    for i in range(1, VIRT):
        turn_copy(i).wait_recv()
    for nb in range(spans):
        at = slice(nb * SPAN, (nb + 1) * SPAN)
        own = lax.dot_general(
            diagonal, jnp.concatenate(split_two(turned[nb]), axis=0), NT, preferred_element_type=F32)
        result[at, :] = lax.dot_general(own.astype(BF16), own_lanes, NN, preferred_element_type=F32)

    def out_copy(t):
        at = pl.ds(t * 128, 128)
        return pltpu.make_async_copy(result.at[at], out.at[at], out_sem.at[t])

    for copy in chip_copies + [c for pair in starts for c in pair] + list(direct + forward):
        copy.wait_send()
    for i in range(1, VIRT):
        turn_copy(i).wait_send()
        look_copy(i).wait_send()

    some = n_pair // GROUPS
    pad = jnp.zeros((some, PAD - slots, BLOCK), F32)
    for g in range(GROUPS):
        for i in range(g * some, min((g + 1) * some, n_pair - 1)):
            pair_copy(i).wait_recv()
        rows_in = jnp.concatenate([came[g * some:(g + 1) * some], pad], axis=1).reshape(some * PAD, BLOCK)
        rows_in = jnp.concatenate(split_two(rows_in), axis=1)
        for t in range(tiles):
            at = slice(t * 128, (t + 1) * 128)
            fetched = lax.dot_general(
                take_one[at, g * some * PAD:(g + 1) * some * PAD], rows_in, NN, preferred_element_type=F32)
            result[at, :] += lax.dot_general(fetched.astype(BF16), mirror_lanes, NN, preferred_element_type=F32)
            if g == GROUPS - 1:
                out_copy(t).start()
    for i in range(n_pair - 1):
        pair_copy(i).wait_send()
    for t in range(tiles):
        out_copy(t).wait()


def per_device(n_pair, slots, amplitudes, integrals, mask, slab, owner):
    rows, cs, width = amplitudes.shape
    dma = pltpu.SemaphoreType.DMA
    n_slots = n_pair * PAD
    spans = rows // SPAN
    anywhere = pl.BlockSpec(memory_space=pl.ANY)
    return pl.pallas_call(
        functools.partial(kernel, n_pair, slots),
        out_shape=jax.ShapeDtypeStruct((rows, BLOCK), F32),
        in_specs=[anywhere, anywhere, anywhere, pl.BlockSpec(memory_space=pltpu.SMEM), anywhere],
        out_specs=anywhere,
        scratch_shapes=[
            pltpu.VMEM((rows, cs, width), BF16),
            pltpu.VMEM((rows, cs * width), BF16),
            pltpu.VMEM((NX, 32, CORES * 4, cs, width), BF16),
            pltpu.VMEM((2, CORES * BLOCK, cs * width), BF16),
            pltpu.VMEM((NX, spans, CORES, BLOCK, SPAN), F32),
            pltpu.VMEM((NX, spans, BLOCK, SPAN), F32),
            pltpu.VMEM((NX, spans, BLOCK, SPAN), F32),
            pltpu.VMEM((2, spans, HALF, SPAN), F32),
            pltpu.VMEM((spans, BLOCK, SPAN), F32),
            pltpu.VMEM((spans, BLOCK, SPAN), F32),
            pltpu.VMEM((spans, BLOCK, SPAN), F32),
            pltpu.VMEM((n_slots, 2 * BLOCK), F32),
            pltpu.VMEM((n_pair, slots, BLOCK), F32),
            pltpu.VMEM((n_pair, slots, BLOCK), F32),
            pltpu.VMEM((n_slots, rows), BF16),
            pltpu.VMEM((rows, n_slots), BF16),
            pltpu.VMEM((16, 2, rows), jnp.int32),
            pltpu.VMEM((n_pair * rows // 128, 128), jnp.int32),
            pltpu.VMEM((rows, BLOCK), F32),
            pltpu.VMEM((VIRT, 8, 128), F32),
            dma((rows // 128,)),
            dma((NX,)),
            dma((2,)),
            dma((rows // 128,)),
            dma((NX, spans)),
            dma((NX, spans)),
            dma((6, spans)),
            dma((6, spans)),
            dma((VIRT,)),
            dma((VIRT,)),
            dma((n_pair,)),
            dma((n_pair,)),
            dma((VIRT,)),
            dma((VIRT,)),
        ],
        compiler_params=pltpu.CompilerParams(
            collective_id=0, has_side_effects=True, vmem_limit_bytes=56 * 2**20),
        cost_estimate=pl.CostEstimate(
            flops=2 * rows * cs * width * VIRT * BLOCK, bytes_accessed=13 * 2**20, transcendentals=0),
    )(amplitudes, integrals.reshape(32, 32, cs, width), jnp.transpose(mask, (1, 2, 0)), slab, owner.reshape(-1, 128))


def solution(mesh, slots=17):
    return jax.shard_map(
        functools.partial(per_device, mesh.shape["pair"], slots),
        mesh=mesh,
        in_specs=(
            P("pair", None, "virt"),
            P(None, None, "virt"),
            P("pair", None, "virt"),
            P(),
            P(),
        ),
        out_specs=P("pair", "virt"),
        check_vma=False,
    )
```

```python
import functools

import jax
import jax.numpy as jnp
from jax import lax
from jax.experimental import pallas as pl
from jax.experimental.pallas import tpu as pltpu
from jax.sharding import PartitionSpec as P

MESH = pl.DeviceIdType.MESH
F32 = jnp.float32
BF16 = jnp.bfloat16
NX = 4
CORES = 2
VIRT = NX * CORES
BLOCK = 128
PAD = 24
NZ = 8
NT = (((1,), (1,)), ((), ()))
NN = (((1,), (0,)), ((), ()))


def split_two(value):
    high = value.astype(BF16)
    return high, (value - high.astype(F32)).astype(BF16)


def iota(shape, dim):
    return lax.broadcasted_iota(jnp.int32, shape, dim)


def flatten_into(dst, row, block, cs, width):
    flat = pltpu.einshape("pcd->p(cd)", block)
    for j in range(2):
        for c in range(cs):
            at = j * cs * 128 + c * 128
            dst[pl.ds(row, 16), at:at + 128] = flat[:, c * width + j * 128:c * width + (j + 1) * 128]


def kernel(
    n_pair, slots,
    amp, ints, mask_ref, slab_ref, owner_ref, own_ref, fetched_ref,
    amp_raw, amp_flat, int_raw, int_flat, part, chip_in, acc, fwd, fin_left, fin_right,
    turned, sent, came, send_one, take_one,
    amp_sem, int_sem, chip_send, chip_recv, ring_send, ring_recv, turn_send, turn_recv, pair_send, pair_recv,
):
    rows, cs, width = amp_raw.shape
    tiles = rows // 128
    half_k = cs * 128
    half = BLOCK // 2
    me_p = lax.axis_index("pair")
    me_v = lax.axis_index("virt")
    x = me_v // CORES
    core = me_v % CORES
    other = me_v + 1 - 2 * core
    right = ((x + 1) % NX) * CORES + core
    left = ((x + NX - 1) % NX) * CORES + core

    def fetch_amp(q):
        at = pl.ds(q * 128, 128)
        return pltpu.make_async_copy(amp.at[at], amp_raw.at[at], amp_sem.at[q])

    def fetch_ints(s):
        to = (x + (2, 1, 3, 0)[s]) % NX
        return pltpu.make_async_copy(ints.at[:, pl.ds(to * CORES * 4, CORES * 4)], int_raw.at[s], int_sem.at[s])

    for q in range(tiles):
        fetch_amp(q).start()
    fetch_ints(0).start()

    barrier = pltpu.get_barrier_semaphore()

    @pl.loop(1, VIRT)
    def _(i):
        pl.semaphore_signal(barrier, inc=1, device_id=(me_p, (me_v + i) % VIRT), device_id_type=MESH)

    @pl.loop(1, n_pair)
    def _(i):
        pl.semaphore_signal(barrier, inc=1, device_id=((me_p + i) % n_pair, me_v), device_id_type=MESH)

    for q in range(tiles):
        fetch_amp(q).wait()

        @pl.loop(0, 8, unroll=4)
        def _(g):
            row = pl.multiple_of(q * 128 + g * 16, 16)
            flatten_into(amp_flat, row, amp_raw[pl.ds(row, 16)], cs, width)

    for s in range(1, NX):
        fetch_ints(s).start()
    select = mask_ref[slab_ref[0] // 8].astype(F32)
    runs = (((0, 0), (0, 4)), ((1, 4), (2, 0)), ((1, 0), (2, 4)), ((3, 0), (3, 4)))

    def arrange(k):
        flat = int_flat.at[k % 2]
        for c in range(CORES):
            for r in range(2):
                s, first = runs[k][r]

                @pl.loop(0, 4, unroll=4)
                def _(g):
                    block = jnp.concatenate(
                        [int_raw[s, (first + g) * 4 + a, pl.ds(c * 4, 4)] for a in range(4)], axis=0)
                    row = pl.multiple_of((c * 8 + r * 4 + g) * 16, 16)
                    flatten_into(flat, row, block, cs, width)

    def multiply(k, nb):
        flat = int_flat.at[k % 2]
        span = min(256, rows)
        ps = slice(nb * span, (nb + 1) * span)
        one = lax.dot_general(flat[:, :half_k], amp_flat[ps, :half_k], NT, preferred_element_type=F32)
        two = lax.dot_general(flat[:, half_k:], amp_flat[ps, half_k:], NT, preferred_element_type=F32)
        value = one * select[0:1, ps] + two * select[1:2, ps]
        for c in range(CORES):
            part[k, c, :, ps] = value[c * BLOCK:(c + 1) * BLOCK]

    later = range(1, rows // min(256, rows))

    def chip_copy(k):
        return pltpu.make_async_remote_copy(
            src_ref=part.at[k, 1 - core], dst_ref=chip_in.at[k], send_sem=chip_send.at[k], recv_sem=chip_recv.at[k],
            device_id=(me_p, other), device_id_type=MESH)

    def ring_copy(i, src, dst, to):
        return pltpu.make_async_remote_copy(
            src_ref=src, dst_ref=dst, send_sem=ring_send.at[i], recv_sem=ring_recv.at[i],
            device_id=(me_p, to), device_id_type=MESH)

    low, high = pl.ds(0, half), pl.ds(half, half)
    ring = [
        ring_copy(0, acc.at[0, low], fwd.at[0], right),
        ring_copy(1, acc.at[0, high], fwd.at[1], left),
        ring_copy(2, acc.at[1, low], fin_left.at[high], right),
        ring_copy(3, acc.at[1, high], fin_right.at[low], left),
        ring_copy(4, acc.at[2, low], fin_left.at[low], right),
        ring_copy(5, acc.at[2, high], fin_right.at[high], left),
    ]

    def chip_sum(k):
        chip_copy(k).wait_recv()
        acc[k] = part[k, core] + chip_in[k]

    fetch_ints(0).wait()
    arrange(0)
    multiply(0, 0)
    for nb in later:
        multiply(0, nb)
    pl.semaphore_wait(barrier, VIRT - 1 + n_pair - 1)
    chip_copy(0).start()
    fetch_ints(1).wait()
    fetch_ints(2).wait()
    arrange(1)
    multiply(1, 0)
    chip_sum(0)
    ring[0].start()
    ring[1].start()
    for nb in later:
        multiply(1, nb)
    chip_copy(1).start()
    arrange(2)
    multiply(2, 0)
    chip_sum(1)
    ring[2].start()
    ring[3].start()
    for nb in later:
        multiply(2, nb)
    chip_copy(2).start()
    fetch_ints(3).wait()
    arrange(3)
    multiply(3, 0)
    chip_sum(2)
    for nb in later:
        multiply(3, nb)
    chip_copy(3).start()
    ring[0].wait_recv()
    acc[2, low] += fwd[0]
    ring[4].start()
    ring[1].wait_recv()
    acc[2, high] += fwd[1]
    ring[5].start()

    eye = iota((128, 128), 0) == iota((128, 128), 1)

    def as_column(row):
        return jnp.sum(jnp.where(eye, row, 0.0), axis=1, keepdims=True)

    def as_row(column):
        return jnp.sum(jnp.where(eye, column, 0.0), axis=0, keepdims=True)

    own_rows = [owner_ref[pl.ds(me_p * tiles + t, 1), :] for t in range(tiles)]
    wanted = [as_column((r ^ 1).astype(F32)).astype(jnp.int32) for r in own_rows]
    order_rows = [(r // 2).astype(F32) for r in own_rows]
    order_columns = [as_column(r) for r in order_rows]
    there_columns = []
    for t in range(tiles):
        want = jnp.broadcast_to(wanted[t], (128, 128))

        def look(g, found):
            return jnp.where(owner_ref[pl.ds(g, 1), :] == want, g // tiles, found)

        found = lax.fori_loop(0, n_pair * tiles, look, jnp.zeros((128, 128), jnp.int32), unroll=4)
        there_columns.append(jnp.max(found.astype(F32), axis=1, keepdims=True))
    there_rows = [as_row(c) for c in there_columns]
    places = []
    for t in range(tiles):
        before = jnp.zeros((128, 128), F32)
        for u in range(tiles):
            hit = (there_rows[u] == there_columns[t]) & (order_rows[u] < order_columns[t])
            before = before + jnp.where(hit, 1.0, 0.0)
        places.append(there_columns[t] * PAD + jnp.sum(before, axis=1, keepdims=True))
    n_slots = n_pair * PAD
    for t in range(tiles):
        at = slice(t * 128, (t + 1) * 128)
        column = places[t].astype(jnp.int32)
        take_one[at, :] = jnp.where(iota((128, n_slots), 1) == column, 1.0, 0.0).astype(BF16)
        row = as_row(places[t]).astype(jnp.int32)
        send_one[:, at] = jnp.where(iota((n_slots, 128), 0) == row, 1.0, 0.0).astype(BF16)

    came[pl.ds(me_p, 1)] = jnp.zeros((1, slots, BLOCK), F32)
    source, target = iota((BLOCK, BLOCK), 0), iota((BLOCK, BLOCK), 1)
    group, first, second = source // 16, (source // 4) % 4, source % 4
    own_lanes = jnp.where(target == first * 32 + group * 4 + second, 1.0, 0.0).astype(BF16)
    mirror_lanes = jnp.where(target == second * 32 + group * 4 + first, 1.0, 0.0).astype(BF16)
    own_lanes = jnp.concatenate([own_lanes, own_lanes], axis=0)
    mirror_lanes = jnp.concatenate([mirror_lanes, mirror_lanes], axis=0)
    diagonal = jnp.where(iota((rows, rows), 0) == iota((rows, rows), 1), 1.0, 0.0).astype(BF16)

    chip_sum(3)
    for i in range(2, 6):
        ring[i].wait_recv()
    acc[3] = acc[3] + fin_left[...] + fin_right[...]
    sum_high, sum_low = split_two(acc[3])
    both = lax.dot_general(
        send_one[...], jnp.concatenate([sum_high, sum_low], axis=0), NT, preferred_element_type=F32)
    sent[...] = (both[:, :BLOCK] + both[:, BLOCK:]).reshape(n_pair, PAD, BLOCK)[:, :slots]

    steps = [(dy, dz) for dy in range(n_pair // NZ) for dz in range(NZ) if dy or dz]
    steps.sort(key=lambda s: (-min(s[0], n_pair // NZ - s[0]) - min(s[1], NZ - s[1]), s))

    def pair_copy(i):
        dy, dz = steps[i]
        to = ((me_p // NZ + dy) % (n_pair // NZ)) * NZ + (me_p + dz) % NZ
        return pltpu.make_async_remote_copy(
            src_ref=sent.at[to], dst_ref=came.at[me_p], send_sem=pair_send.at[i], recv_sem=pair_recv.at[i],
            device_id=(to, me_v), device_id_type=MESH)

    for i in range(n_pair - 1):
        pair_copy(i).start()

    def turn_copy(i):
        to = (me_v + i) % VIRT
        src = acc.at[3, pl.ds(pl.multiple_of(to * 16, 16), 16)]
        dst = turned.at[pl.ds(pl.multiple_of(me_v * 16, 16), 16)]
        return pltpu.make_async_remote_copy(
            src_ref=src, dst_ref=dst, send_sem=turn_send.at[i], recv_sem=turn_recv.at[i],
            device_id=(me_p, to), device_id_type=MESH)

    for i in range(1, VIRT):
        turn_copy(i).start()
    mine = pl.ds(pl.multiple_of(me_v * 16, 16), 16)
    turned[mine, :] = acc[3, mine, :]
    for i in range(1, VIRT):
        turn_copy(i).wait_recv()
    own_high, own_low = split_two(turned[...])
    own_pair = lax.dot_general(diagonal, jnp.concatenate([own_high, own_low], axis=0), NT, preferred_element_type=F32)
    own_ref[...] = lax.dot_general(own_pair.astype(BF16), own_lanes, NN, preferred_element_type=F32)

    for k in range(NX):
        chip_copy(k).wait_send()
    for copy in ring:
        copy.wait_send()
    for i in range(1, VIRT):
        turn_copy(i).wait_send()
    for i in range(n_pair - 1):
        pair_copy(i).wait_send()
    for i in range(n_pair - 1):
        pair_copy(i).wait_recv()

    rest = jnp.zeros((n_pair, PAD - slots, BLOCK), F32)
    came_high, came_low = split_two(jnp.concatenate([came[...], rest], axis=1).reshape(n_slots, BLOCK))
    fetched = lax.dot_general(
        take_one[...], jnp.concatenate([came_high, came_low], axis=1), NN, preferred_element_type=F32)
    fetched_ref[...] = lax.dot_general(fetched.astype(BF16), mirror_lanes, NN, preferred_element_type=F32)


def per_device(n_pair, slots, amplitudes, integrals, mask, slab, owner):
    rows, cs, width = amplitudes.shape
    dma = pltpu.SemaphoreType.DMA
    n_slots = n_pair * PAD
    half = BLOCK // 2
    own, fetched = pl.pallas_call(
        functools.partial(kernel, n_pair, slots),
        out_shape=[jax.ShapeDtypeStruct((rows, BLOCK), F32)] * 2,
        in_specs=[
            pl.BlockSpec(memory_space=pl.ANY),
            pl.BlockSpec(memory_space=pl.ANY),
            pl.BlockSpec(memory_space=pltpu.VMEM),
            pl.BlockSpec(memory_space=pltpu.SMEM),
            pl.BlockSpec(memory_space=pltpu.VMEM),
        ],
        out_specs=[pl.BlockSpec(memory_space=pltpu.VMEM)] * 2,
        scratch_shapes=[
            pltpu.VMEM((rows, cs, width), BF16),
            pltpu.VMEM((rows, cs * width), BF16),
            pltpu.VMEM((NX, 32, CORES * 4, cs, width), BF16),
            pltpu.VMEM((2, CORES * BLOCK, cs * width), BF16),
            pltpu.VMEM((NX, CORES, BLOCK, rows), F32),
            pltpu.VMEM((NX, BLOCK, rows), F32),
            pltpu.VMEM((NX, BLOCK, rows), F32),
            pltpu.VMEM((2, half, rows), F32),
            pltpu.VMEM((BLOCK, rows), F32),
            pltpu.VMEM((BLOCK, rows), F32),
            pltpu.VMEM((BLOCK, rows), F32),
            pltpu.VMEM((n_pair, slots, BLOCK), F32),
            pltpu.VMEM((n_pair, slots, BLOCK), F32),
            pltpu.VMEM((n_slots, rows), BF16),
            pltpu.VMEM((rows, n_slots), BF16),
            dma((rows // 128,)),
            dma((NX,)),
            dma((NX,)),
            dma((NX,)),
            dma((6,)),
            dma((6,)),
            dma((VIRT,)),
            dma((VIRT,)),
            dma((n_pair,)),
            dma((n_pair,)),
        ],
        compiler_params=pltpu.CompilerParams(
            collective_id=0, has_side_effects=True, vmem_limit_bytes=56 * 2**20),
        cost_estimate=pl.CostEstimate(
            flops=2 * rows * cs * width * VIRT * BLOCK, bytes_accessed=13 * 2**20, transcendentals=0),
    )(amplitudes, integrals.reshape(32, 32, cs, width), jnp.transpose(mask, (1, 2, 0)), slab, owner.reshape(-1, 128))
    return own + fetched


def solution(mesh, slots=17):
    return jax.shard_map(
        functools.partial(per_device, mesh.shape["pair"], slots),
        mesh=mesh,
        in_specs=(
            P("pair", None, "virt"),
            P(None, None, "virt"),
            P("pair", None, "virt"),
            P(),
            P(),
        ),
        out_specs=P("pair", "virt"),
        check_vma=False,
    )
```
